32 devices in a mesh: seqa: 8 (over y, x, core), seqb: 4 (over z).
Axes of the slice: x: 2, y: 2, z: 4, core: 2. Of those that a mesh axis runs over, the one named last changes fastest.
Arguments:
- hidden_in: bfloat16 [4096, 2880], P(('seqa', 'seqb')), may hold values from -6 to 6
- queries: bfloat16 [4096, 4096], P(('seqa', 'seqb')), may hold values from -200 to 200
- grad_out: bfloat16 [4096, 4096], P(('seqa', 'seqb')), may hold values from -5 to 5
- key_weight: bfloat16 [2880, 512], P(None, ('seqa', 'seqb')), may hold values from -0.109375 to 0.109375
- value_weight: bfloat16 [2880, 512], P(None, ('seqa', 'seqb')), may hold values from -0.109375 to 0.109375
Outputs:
- grad_queries: bfloat16 [4096, 4096], P(('seqa', 'seqb'))
- grad_keys: bfloat16 [4096, 512], P(('seqa', 'seqb'))
- grad_values: bfloat16 [4096, 512], P(('seqa', 'seqb'))
- grad_inputs: bfloat16 [4096, 2880], P(('seqa', 'seqb'))
- grad_key_weight: float32 [2880, 512], P(None, ('seqa', 'seqb'))
- grad_value_weight: float32 [2880, 512], P(None, ('seqa', 'seqb'))
The draws below stay inside these ranges and needn't reach their ends.
All inputs are finite; a program needn't handle non-finite values.
Results may differ from the reference program's by a relative error of at most 0.011.
Values may be sent and summed in bfloat16 or wider, within the bound.
No kernel may reach another device: no remote copies, remote signals or barrier semaphores. Data moves between devices by JAX's collectives and lax.ppermute only.
A program may use at most 128 MiB of HBM per device.

```python
import jax
import jax.numpy as jnp
from jax import lax

D = 2880
KV_HEADS = 8
HEAD = 64
WIN = 128
TOK_DEV = 128
TOKENS = 4096
QW = 4096
KVW = 512


def draw_queries(key, part):
    base = jnp.clip(jax.random.normal(key, (TOKENS, QW), jnp.float32), -5.0, 5.0)
    return base.astype(jnp.bfloat16)


def draw_grad_out(key, part):
    base = jnp.clip(jax.random.normal(jax.random.fold_in(key, 7), (TOKENS, QW), jnp.float32), -5.0, 5.0)
    return base.astype(jnp.bfloat16)


def steps_of(rng, dims, shards, smallest, high):
    gain = 1.0
    for position, parts in shards:
        steps = jax.random.uniform(jax.random.fold_in(jax.random.fold_in(rng, 6), position), (parts,), jnp.float32, smallest / len(shards), high / len(shards))
        gain = gain * jnp.repeat(jnp.exp(steps), dims[position] // parts).reshape((-1,) + (1,) * (len(dims) - 1 - position))
    return gain


def centred(stream_key, shape, scale, bound, shards=(), held_as=jnp.bfloat16):
    loudness = steps_of(stream_key, shape, shards, -0.22, 0.18) if shards else 1.0
    entries = jax.random.normal(stream_key, shape, jnp.float32) * scale * loudness
    return jnp.minimum(jnp.maximum(entries, -bound), bound).astype(held_as)


def setup_inputs(seed: int = 0) -> dict:
    streams_of = jax.random.split(jax.random.key(seed), 6)
    hidden_in = centred(streams_of[0], (TOKENS, D), 1.0, 6.0, ((0, 32),))
    queries = draw_queries(jax.random.fold_in(streams_of[5], 71), 0)
    grad_out = draw_grad_out(jax.random.fold_in(streams_of[5], 71), 0)
    key_weight = centred(streams_of[3], (D, KVW), D ** -0.5, 0.109375, ((1, 32),))
    value_weight = centred(streams_of[4], (D, KVW), D ** -0.5, 0.109375, ((1, 32),))
    return dict(hidden_in=hidden_in, queries=queries, grad_out=grad_out, key_weight=key_weight, value_weight=value_weight)


def lowered(value):
    return lax.optimization_barrier(value.astype(jnp.bfloat16))


def head_group(query_rows, grad_rows, key_rows, value_rows, allowed):
    count = query_rows.shape[0]
    width = key_rows.shape[1]
    group = query_rows.shape[1] // width
    factor = width ** -0.5
    query_heads = query_rows.reshape(count, group, width).astype(jnp.float32)
    grad_heads = grad_rows.reshape(count, group, width).astype(jnp.float32)
    key_wide = key_rows.astype(jnp.float32)
    value_wide = value_rows.astype(jnp.float32)
    scores = jnp.einsum("tgh,lh->gtl", query_heads, key_wide) * factor
    masked = jnp.where(allowed[None], scores, -1e30)
    peak = jnp.max(masked, axis=2, keepdims=True)
    weights = jnp.where(allowed[None], jnp.exp(masked - peak), 0.0)
    weights = weights / jnp.sum(weights, axis=2, keepdims=True)
    weights_low = lowered(weights).astype(jnp.float32)
    attended = lowered(jnp.einsum("gtl,lh->tgh", weights_low, value_wide)).astype(jnp.float32)
    delta = jnp.sum(grad_heads * attended, axis=2)
    grad_weights = jnp.einsum("tgh,lh->gtl", grad_heads, value_wide)
    grad_scores = lowered(weights * (grad_weights - jnp.transpose(delta)[:, :, None])).astype(jnp.float32)
    grad_query = jnp.einsum("gtl,lh->tgh", grad_scores, key_wide) * factor
    grad_key = jnp.einsum("gtl,tgh->lh", grad_scores, query_heads) * factor
    grad_value = jnp.einsum("gtl,tgh->lh", weights_low, grad_heads)
    return grad_query.reshape(count, group * width).astype(jnp.bfloat16), grad_key, grad_value


def reference(hidden_in, queries, grad_out, key_weight, value_weight):
    keys_all = jnp.dot(hidden_in, key_weight, preferred_element_type=jnp.float32).astype(jnp.bfloat16)
    values_all = jnp.dot(hidden_in, value_weight, preferred_element_type=jnp.float32).astype(jnp.bfloat16)
    front = jnp.zeros((WIN, KVW), keys_all.dtype)
    padded_keys = jnp.concatenate([front, keys_all], axis=0)
    padded_values = jnp.concatenate([front, values_all], axis=0)
    span = TOK_DEV + WIN

    def one_block(index):
        start = (index * TOK_DEV).astype(jnp.int32)
        query_rows = lax.dynamic_slice_in_dim(queries, start, TOK_DEV, 0)
        grad_rows = lax.dynamic_slice_in_dim(grad_out, start, TOK_DEV, 0)
        key_rows = lax.dynamic_slice_in_dim(padded_keys, start, span, 0)
        value_rows = lax.dynamic_slice_in_dim(padded_values, start, span, 0)
        query_pos = start + jnp.arange(TOK_DEV, dtype=jnp.int32)
        key_pos = start - WIN + jnp.arange(span, dtype=jnp.int32)
        gap = query_pos[:, None] - key_pos[None, :]
        allowed = (gap >= 0) & (gap <= WIN) & (key_pos[None, :] >= 0)
        query_groups = jnp.moveaxis(query_rows.reshape(TOK_DEV, KV_HEADS, -1), 1, 0)
        grad_groups = jnp.moveaxis(grad_rows.reshape(TOK_DEV, KV_HEADS, -1), 1, 0)
        key_groups = jnp.moveaxis(key_rows.reshape(span, KV_HEADS, HEAD), 1, 0)
        value_groups = jnp.moveaxis(value_rows.reshape(span, KV_HEADS, HEAD), 1, 0)
        grad_query, grad_key, grad_value = lax.map(
            lambda items: head_group(items[0], items[1], items[2], items[3], allowed),
            (query_groups, grad_groups, key_groups, value_groups))
        return (jnp.moveaxis(grad_query, 0, 1).reshape(TOK_DEV, QW),
                jnp.moveaxis(grad_key, 0, 1).reshape(span, KVW),
                jnp.moveaxis(grad_value, 0, 1).reshape(span, KVW))

    block_count = TOKENS // TOK_DEV
    grad_query, grad_key, grad_value = lax.map(one_block, jnp.arange(block_count, dtype=jnp.int32))

    def combine(blocks):
        own_part = blocks[:, WIN:]
        later = jnp.concatenate([blocks[1:, :WIN], jnp.zeros_like(blocks[:1, :WIN])], axis=0)
        merged = jnp.concatenate([own_part[:, :TOK_DEV - WIN], own_part[:, TOK_DEV - WIN:] + later], axis=1)
        return merged.reshape(TOKENS, KVW).astype(jnp.bfloat16)

    grad_queries = grad_query.reshape(TOKENS, QW)
    grad_keys = combine(grad_key)
    grad_values = combine(grad_value)
    contract_cols = (((1,), (1,)), ((), ()))
    grad_inputs = (lax.dot_general(grad_keys, key_weight, contract_cols, preferred_element_type=jnp.float32)
                   + lax.dot_general(grad_values, value_weight, contract_cols, preferred_element_type=jnp.float32)).astype(jnp.bfloat16)
    contract_rows = (((0,), (0,)), ((), ()))
    grad_scale = TOKENS ** -0.5
    grad_key_weight = lax.dot_general(hidden_in, grad_keys, contract_rows, preferred_element_type=jnp.float32) * grad_scale
    grad_value_weight = lax.dot_general(hidden_in, grad_values, contract_rows, preferred_element_type=jnp.float32) * grad_scale
    return grad_queries, grad_keys, grad_values, grad_inputs, grad_key_weight, grad_value_weight
```

```python
import functools
import math

import jax
import jax.numpy as jnp
from jax import lax
from jax.experimental import pallas as pl
from jax.experimental.pallas import tpu as pltpu
from jax.sharding import Mesh, PartitionSpec as P

KV_HEADS = 8
HEAD = 64
WIN = 128
LANES = 128
QUARTERS = 4
SUBLANES = 16

F32 = jnp.float32
BF16 = jnp.bfloat16
NT = (((1,), (1,)), ((), ()))
AXES = ("hi", "x", "c", "z")


def params(megabytes=48):
    return pltpu.CompilerParams(vmem_limit_bytes=megabytes * 1024 * 1024)


def cost(flops, *arrays):
    size = sum(math.prod(a.shape) * a.dtype.itemsize for a in arrays)
    return pl.CostEstimate(flops=int(flops), bytes_accessed=int(size), transcendentals=0)


def struct(shape, dtype):
    return jax.ShapeDtypeStruct(shape, dtype)


VMEM = pl.BlockSpec(memory_space=pltpu.VMEM)
SMEM = pl.BlockSpec(memory_space=pltpu.SMEM)


def padded_pair(block, half):
    lane = lax.broadcasted_iota(jnp.int32, block.shape, 1)
    here = jnp.where(lane // HEAD == half, block.astype(F32), 0.0)
    there = pltpu.roll(here, HEAD, 1)
    even, odd = jnp.where(half == 0, here, there), jnp.where(half == 0, there, here)
    return even.astype(BF16), odd.astype(BF16)


def stacked(own, halo, half):
    own_even, own_odd = padded_pair(own, half)
    halo_even, halo_odd = padded_pair(halo, half)
    return jnp.concatenate([own_even, halo_even, own_odd, halo_odd], axis=0)


def folded(total):
    rows = total.shape[0] // 4
    lane = lax.broadcasted_iota(jnp.int32, (rows, LANES), 1)
    out = []
    for part in range(2):
        even = total[part * rows : (part + 1) * rows]
        odd = total[(2 + part) * rows : (3 + part) * rows]
        both = jnp.where(lane < HEAD, even, odd)
        out.append(both + pltpu.roll(both, HEAD, 1))
    return out


def store_half(ref, value, half):
    lane = lax.broadcasted_iota(jnp.int32, value.shape, 1)
    ref[0] = jnp.where(lane // HEAD == half, value, ref[0].astype(F32)).astype(ref.dtype)


def softmax_kernel(first_ref, q_ref, go_ref, key_ref, halo_ref, probs_ref, diag_ref, own_ref, back_ref):
    rows = key_ref.shape[1]
    u = lax.broadcasted_iota(jnp.int32, (rows, rows), 0)
    t = lax.broadcasted_iota(jnp.int32, (rows, rows), 1)
    later, same = u > t, u == t
    rate = HEAD ** (-0.5) * math.log2(math.e)
    shift = jnp.where(first_ref[0] == 1, -1e30, 0.0).astype(F32)
    half = pl.program_id(1)
    keys = stacked(key_ref[0], halo_ref[0], half)
    total = jnp.zeros((4 * rows, LANES), F32)
    for pair in range(q_ref.shape[1] // LANES):
        cols = slice(pair * LANES, (pair + 1) * LANES)
        scores = lax.dot_general(keys, q_ref[:, cols], NT, preferred_element_type=F32)
        weights = []
        for head in range(2):
            own = scores[2 * head * rows : (2 * head + 1) * rows]
            halo = scores[(2 * head + 1) * rows : (2 * head + 2) * rows] + shift
            mixed = jnp.where(later, halo, own)
            diag = jnp.sum(jnp.where(same, halo, 0.0), axis=0, keepdims=True)
            peak = jnp.maximum(jnp.max(mixed, axis=0, keepdims=True), diag)
            mixed = jnp.exp2((mixed - peak) * rate)
            diag = jnp.exp2((diag - peak) * rate)
            inverse = 1.0 / (jnp.sum(mixed, axis=0, keepdims=True) + diag)
            mixed = mixed * inverse
            diag = diag * inverse
            index = 2 * pair + head
            probs_ref[0, index] = mixed.astype(BF16)
            diag_ref[0, index : index + 1] = diag
            weights.append(jnp.where(later, 0.0, mixed).astype(BF16))
            weights.append(jnp.where(later, mixed, jnp.where(same, diag, 0.0)).astype(BF16))
        total += jnp.dot(
            jnp.concatenate(weights, axis=0), go_ref[:, cols], preferred_element_type=F32
        )
    own, back = folded(total)
    store_half(own_ref, own, half)
    store_half(back_ref, back, half)


def scores_kernel(
    q_ref, go_ref, key_ref, key_halo_ref, value_ref, value_halo_ref, probs_ref, diag_ref,
    gq_ref, own_ref, back_ref,
):
    rows = key_ref.shape[1]
    u = lax.broadcasted_iota(jnp.int32, (rows, rows), 0)
    t = lax.broadcasted_iota(jnp.int32, (rows, rows), 1)
    later, same = u > t, u == t
    factor = HEAD ** (-0.5)
    half = pl.program_id(1)
    keys = stacked(key_ref[0], key_halo_ref[0], half)
    keys_across = keys.astype(F32).T.astype(BF16)
    values = stacked(value_ref[0], value_halo_ref[0], half)
    total = jnp.zeros((4 * rows, LANES), F32)
    for pair in range(q_ref.shape[1] // LANES):
        cols = slice(pair * LANES, (pair + 1) * LANES)
        grads = lax.dot_general(values, go_ref[:, cols], NT, preferred_element_type=F32)
        terms = []
        for head in range(2):
            own = grads[2 * head * rows : (2 * head + 1) * rows]
            halo = grads[(2 * head + 1) * rows : (2 * head + 2) * rows]
            index = 2 * pair + head
            probs = probs_ref[0, index].astype(F32)
            diag = diag_ref[0, index : index + 1]
            mixed = jnp.where(later, halo, own)
            edge = jnp.sum(jnp.where(same, halo, 0.0), axis=0, keepdims=True)
            delta = jnp.sum(probs * mixed, axis=0, keepdims=True) + diag * edge
            mixed = probs * (mixed - delta)
            edge = diag * (edge - delta)
            terms.append(jnp.where(later, 0.0, mixed).astype(BF16))
            terms.append(jnp.where(later, mixed, jnp.where(same, edge, 0.0)).astype(BF16))
        stack = jnp.concatenate(terms, axis=0)
        total += jnp.dot(stack, q_ref[:, cols], preferred_element_type=F32)
        across = jnp.dot(keys_across, stack, preferred_element_type=F32)
        gq_ref[:, cols] = (across.T * factor).astype(BF16)
    own, back = folded(total)
    store_half(own_ref, own * factor, half)
    store_half(back_ref, back * factor, half)


def by_head(array):
    rows, width = array.shape
    return pl.BlockSpec((rows, width // KV_HEADS), lambda q, h: (0, h * QUARTERS + q))


def by_step(array):
    block = (1,) + array.shape[1:]
    return pl.BlockSpec(block, lambda q, h: (2 * q + h,) + (0,) * (len(block) - 1))


def by_quarter(array):
    block = (1,) + array.shape[1:]
    return pl.BlockSpec(block, lambda q, h: (q,) + (0,) * (len(block) - 1))


def softmax_part(first, queries, grad_out, keys, halo):
    rows, width = queries.shape
    group = width // (KV_HEADS * HEAD)
    probs = struct((KV_HEADS, group, rows, rows), BF16)
    diag = struct((KV_HEADS, group, rows), F32)
    sums = struct(keys.shape, F32)
    back = struct(keys.shape, BF16)
    return pl.pallas_call(
        softmax_kernel,
        grid=(QUARTERS, 2),
        in_specs=[SMEM] + [by_head(queries)] * 2 + [by_quarter(keys)] * 2,
        out_specs=[by_step(probs), by_step(diag), by_quarter(sums), by_quarter(back)],
        out_shape=[probs, diag, sums, back],
        compiler_params=params(),
        cost_estimate=cost(8 * rows * rows * width, queries, grad_out, probs),
        name="softmax_part",
    )(first, queries, grad_out, keys, halo)


def scores_part(queries, grad_out, keys, halo, values, value_halo, probs, diag):
    rows, width = queries.shape
    sums = struct(keys.shape, F32)
    back = struct(keys.shape, BF16)
    return pl.pallas_call(
        scores_kernel,
        grid=(QUARTERS, 2),
        in_specs=[by_head(queries)] * 2
        + [by_quarter(keys)] * 4
        + [by_step(probs), by_step(diag)],
        out_specs=[by_head(queries), by_quarter(sums), by_quarter(back)],
        out_shape=[struct(queries.shape, BF16), sums, back],
        compiler_params=params(),
        cost_estimate=cost(12 * rows * rows * width, queries, grad_out, queries, probs),
        name="scores_part",
    )(queries, grad_out, keys, halo, values, value_halo, probs, diag)


def project_kernel(place_ref, *refs):
    pieces, hidden = refs[:8], refs[8:12]
    weight_ref, outs = refs[12], refs[13:]
    hi, z = place_ref[0], place_ref[1]
    step = pieces[0].shape[0]
    depth = len(pieces) // 2
    for r in range(2):
        for k in range(depth):
            row = ((hi ^ r) * depth + (z ^ k)) * step
            weight_ref[pl.ds(pl.multiple_of(row, step), step), :] = pieces[r * depth + k][...]
    weight = weight_ref[...]
    for h_ref, out_ref in zip(hidden, outs):
        across = jnp.dot(weight, h_ref[...], preferred_element_type=F32)
        out_ref[...] = across.T.astype(BF16)


def project(place, pieces, hidden):
    depth, tokens = hidden[0].shape
    cols = sum(p.shape[0] for p in pieces)
    weight = struct((cols, depth), BF16)
    out = struct((tokens, cols), BF16)
    return pl.pallas_call(
        project_kernel,
        in_specs=[SMEM] + [VMEM] * (len(pieces) + len(hidden)),
        out_specs=[VMEM] * (1 + len(hidden)),
        out_shape=[weight] + [out] * len(hidden),
        compiler_params=params(),
        cost_estimate=cost(2 * 4 * tokens * cols * depth, *hidden, weight, weight),
        name="project",
    )(place, *pieces, *hidden)


def arrange_kernel(place_ref, *refs):
    out_ref = refs[-1]
    for r, ref in enumerate(refs[:-1]):
        out_ref[place_ref[2] ^ r] = ref[...]


def arrange(place, parts):
    return pl.pallas_call(
        arrange_kernel,
        in_specs=[SMEM] + [VMEM] * len(parts),
        out_specs=VMEM,
        out_shape=struct((len(parts),) + parts[0].shape, BF16),
        compiler_params=params(),
        name="arrange",
    )(place, *parts)


def natural(quarters):
    lane = lax.broadcasted_iota(jnp.int32, quarters[0].shape, 1)
    blocks = []
    for half in range(2):
        for first in range(0, QUARTERS, 2):
            left, right = quarters[first], quarters[first + 1]
            if half == 0:
                right = pltpu.roll(right, HEAD, 1)
            else:
                left = pltpu.roll(left, HEAD, 1)
            blocks.append(jnp.where(lane < HEAD, left, right))
    return blocks


def finish_kernel(place_ref, own_ref, back_ref, natural_ref, all_ref, *outs):
    quarters = []
    for q in range(QUARTERS):
        total = (own_ref[q] + back_ref[q].astype(F32)).astype(BF16)
        all_ref[q] = total
        quarters.append(total.astype(F32))
    for m, block in enumerate(natural(quarters)):
        natural_ref[:, m * LANES : (m + 1) * LANES] = block.astype(BF16)
    for r, ref in enumerate(outs):
        ref[...] = all_ref[place_ref[2] ^ r]


def finish(place, own, back):
    rows = own.shape[1]
    part = struct(own.shape[1:], BF16)
    return pl.pallas_call(
        finish_kernel,
        in_specs=[SMEM, VMEM, VMEM],
        out_specs=[VMEM] * (2 + QUARTERS),
        out_shape=[struct((rows, QUARTERS * LANES), BF16), struct(own.shape, BF16)]
        + [part] * QUARTERS,
        compiler_params=params(),
        name="finish",
    )(place, own, back)


def spans(size, step):
    return [(at, min(step, size - at)) for at in range(0, size, step)]


def weight_grad_kernel(place_ref, *refs):
    grads, hidden = refs[:4], refs[4:8]
    keep_ref, send_ref, wide_ref = refs[8:]
    hi, z = place_ref[0], place_ref[1]
    for at, size in spans(hidden[0].shape[0], 256):
        total = jnp.zeros((size, grads[0].shape[1]), F32)
        for g_ref, h_ref in zip(grads, hidden):
            total += jnp.dot(h_ref[at : at + size, :], g_ref[...], preferred_element_type=F32)
        wide_ref[:, at : at + size] = total.T
    depth, step = keep_ref.shape[:2]
    for k in range(depth):
        for r, ref in enumerate((keep_ref, send_ref)):
            row = ((hi ^ r) * depth + (z ^ k)) * step
            ref[k] = wide_ref[pl.ds(pl.multiple_of(row, step), step), :].astype(BF16)


def weight_grad(place, grads, hidden, depth):
    size, tokens = hidden[0].shape
    cols = grads[0].shape[1]
    part = struct((depth, cols // (2 * depth), size), BF16)
    return pl.pallas_call(
        weight_grad_kernel,
        in_specs=[SMEM] + [VMEM] * 8,
        out_specs=[VMEM] * 2,
        out_shape=[part] * 2,
        scratch_shapes=[pltpu.VMEM((cols, size), F32)],
        compiler_params=params(),
        cost_estimate=cost(2 * 4 * tokens * cols * size, *hidden, part, part),
        name="weight_grad",
    )(place, *grads, *hidden)


def input_grad_kernel(place_ref, key_ref, value_ref, *refs):
    out_ref = refs[-1]
    weights = (refs[:QUARTERS], refs[QUARTERS:-1])
    for at, size in spans(out_ref.shape[0], 256):
        total = jnp.zeros((key_ref.shape[1], size), F32)
        for grad_ref, group in zip((key_ref, value_ref), weights):
            for r, w_ref in enumerate(group):
                total += jnp.dot(
                    grad_ref[place_ref[2] ^ r],
                    w_ref[:, at : at + size],
                    preferred_element_type=F32,
                )
        out_ref[at : at + size, :] = total.T.astype(BF16)


def input_grad(place, key_all, value_all, key_weights, value_weights):
    cols, size = key_weights[0].shape
    rows = key_all.shape[1]
    out = struct((size, rows), BF16)
    return pl.pallas_call(
        input_grad_kernel,
        in_specs=[SMEM] + [VMEM] * 10,
        out_specs=VMEM,
        out_shape=out,
        compiler_params=params(),
        cost_estimate=cost(16 * rows * cols * size, *key_weights, *value_weights, out),
        name="input_grad",
    )(place, key_all, value_all, *key_weights, *value_weights)


def flip(array, axis, by):
    return lax.ppermute(array, axis, [(i, i ^ by) for i in range(lax.axis_size(axis))])


def flip_group(array, by):
    return lax.ppermute(array, ("x", "c"), [(i, i ^ by) for i in range(QUARTERS)])


def shifted(array, by):
    size = lax.axis_size(AXES)
    pairs = [(i, i + by) for i in range(size) if 0 <= i + by < size]
    return lax.ppermute(array, AXES, pairs)


def gathered(weight):
    depth = lax.axis_size("z")
    mine = [weight] + [flip(weight, "z", k) for k in range(1, depth)]
    return mine + [flip(piece, "hi", 1) for piece in mine]


def scattered(keep, send):
    got = flip(send, "hi", 1)
    total = keep.astype(F32) + got.astype(F32)
    depth = total.shape[0]
    result = total[0]
    for k in range(1, depth):
        result = result + flip(total[k].astype(BF16), "z", k).astype(F32)
    return result


def fast_shards(hidden_in, queries, grad_out, key_weight, value_weight):
    here = lax.axis_index(AXES)
    group = lax.axis_index(("x", "c"))
    place = jnp.stack([lax.axis_index("hi"), lax.axis_index("z"), group]).astype(jnp.int32)
    first = (here == 0).astype(jnp.int32).reshape(1)
    own = hidden_in.T
    across = flip(own, "x", 1)
    hidden = [own, flip(own, "c", 1), across, flip(across, "c", 1)]
    depth = lax.axis_size("z")
    key_pieces = gathered(key_weight.T)
    value_pieces = gathered(value_weight.T)

    def projected(pieces):
        weight, *parts = project(place, pieces, hidden)
        parts = [parts[0]] + [flip_group(parts[r], r) for r in range(1, QUARTERS)]
        rows = arrange(place, parts)
        return weight, rows, shifted(rows, 1)

    key_mine, keys, key_halo = projected(key_pieces)
    value_mine, values, value_halo = projected(value_pieces)

    def filled(mine):
        x_side = flip(mine, "x", 1)
        return [mine, flip(mine, "c", 1), x_side, flip(x_side, "c", 1)]

    key_weights, value_weights = filled(key_mine), filled(value_mine)
    probs, diag, value_own, value_back = softmax_part(first, queries, grad_out, keys, key_halo)

    def finished(sums, back):
        rows, every, *parts = finish(place, sums, shifted(back, -1))
        parts = [parts[0]] + [flip_group(parts[r], r) for r in range(1, QUARTERS)]
        return rows, every, scattered(*weight_grad(place, parts, hidden, depth))

    grad_values, value_every, value_total = finished(value_own, value_back)
    grad_queries, key_own, key_back = scores_part(
        queries, grad_out, keys, key_halo, values, value_halo, probs, diag
    )
    grad_keys, key_every, key_total = finished(key_own, key_back)
    grad_inputs = input_grad(place, key_every, value_every, key_weights, value_weights).T
    scale = (hidden_in.shape[0] * lax.axis_size(AXES)) ** (-0.5)
    return (
        grad_queries,
        grad_keys,
        grad_values,
        grad_inputs,
        (key_total * scale).T,
        (value_total * scale).T,
    )


def to_quarters(rows):
    count = rows.shape[0]
    split = rows.reshape(count, 2, QUARTERS, HEAD)
    return jnp.transpose(split, (2, 0, 1, 3)).reshape(QUARTERS, count, 2 * HEAD)


def from_quarters(quarters):
    count = quarters.shape[1]
    split = quarters.reshape(QUARTERS, count, 2, HEAD)
    return jnp.transpose(split, (1, 2, 0, 3)).reshape(count, 2 * QUARTERS * HEAD)


def plain_shards(hidden_in, queries, grad_out, key_weight, value_weight):
    key_full = lax.all_gather(key_weight.T, AXES, axis=0, tiled=True)
    value_full = lax.all_gather(value_weight.T, AXES, axis=0, tiled=True)
    first = (lax.axis_index(AXES) == 0).astype(jnp.int32).reshape(1)

    def rows_of(weight):
        rows = lax.dot_general(hidden_in, weight, NT, preferred_element_type=F32)
        return to_quarters(rows.astype(BF16))

    keys, values = rows_of(key_full), rows_of(value_full)
    key_halo, value_halo = shifted(keys, 1), shifted(values, 1)
    probs, diag, value_own, value_back = softmax_part(first, queries, grad_out, keys, key_halo)
    grad_queries, key_own, key_back = scores_part(
        queries, grad_out, keys, key_halo, values, value_halo, probs, diag
    )
    grad_keys = from_quarters(key_own + shifted(key_back, -1)).astype(BF16)
    grad_values = from_quarters(value_own + shifted(value_back, -1)).astype(BF16)
    grad_inputs = (
        jnp.dot(grad_keys, key_full, preferred_element_type=F32)
        + jnp.dot(grad_values, value_full, preferred_element_type=F32)
    ).astype(BF16)
    scale = (hidden_in.shape[0] * lax.axis_size(AXES)) ** (-0.5)

    def summed(grad):
        rows = (((0,), (0,)), ((), ()))
        part = lax.dot_general(grad, hidden_in, rows, preferred_element_type=F32)
        return (lax.psum_scatter(part, AXES, scatter_dimension=0, tiled=True) * scale).T

    return (
        grad_queries,
        grad_keys,
        grad_values,
        grad_inputs,
        summed(grad_keys),
        summed(grad_values),
    )


def solution(mesh):
    outer, inner = mesh.shape["seqa"], mesh.shape["seqb"]
    split = Mesh(mesh.devices.reshape(outer // QUARTERS, 2, 2, inner), AXES)
    cols = KV_HEADS * HEAD // (outer * inner)
    fast = outer == 2 * QUARTERS and inner & (inner - 1) == 0 and cols % SUBLANES == 0
    rows, columns = P(AXES, None), P(None, AXES)
    return jax.shard_map(
        fast_shards if fast else plain_shards,
        mesh=split,
        in_specs=(rows, rows, rows, columns, columns),
        out_specs=(rows, rows, rows, rows, columns, columns),
        check_vma=False,
    )
```

```python
import functools
import math

import jax
import jax.numpy as jnp
from jax import lax
from jax.experimental import pallas as pl
from jax.experimental.pallas import tpu as pltpu
from jax.sharding import Mesh, PartitionSpec as P

KV_HEADS = 8
HEAD = 64
WIN = 128
LANES = 128
QUARTERS = 4
SUBLANES = 16

F32 = jnp.float32
BF16 = jnp.bfloat16
NT = (((1,), (1,)), ((), ()))
AXES = ("hi", "x", "c", "z")


def params(megabytes=48):
    return pltpu.CompilerParams(vmem_limit_bytes=megabytes * 1024 * 1024)


def cost(flops, *arrays):
    size = sum(math.prod(a.shape) * a.dtype.itemsize for a in arrays)
    return pl.CostEstimate(flops=int(flops), bytes_accessed=int(size), transcendentals=0)


def struct(shape, dtype):
    return jax.ShapeDtypeStruct(shape, dtype)


VMEM = pl.BlockSpec(memory_space=pltpu.VMEM)
SMEM = pl.BlockSpec(memory_space=pltpu.SMEM)


def padded_pair(block, half):
    lane = lax.broadcasted_iota(jnp.int32, block.shape, 1)
    here = jnp.where(lane // HEAD == half, block.astype(F32), 0.0)
    there = pltpu.roll(here, HEAD, 1)
    even, odd = jnp.where(half == 0, here, there), jnp.where(half == 0, there, here)
    return even.astype(BF16), odd.astype(BF16)


def stacked(own, halo, half):
    own_even, own_odd = padded_pair(own, half)
    halo_even, halo_odd = padded_pair(halo, half)
    return jnp.concatenate([own_even, halo_even, own_odd, halo_odd], axis=0)


def folded(total):
    rows = total.shape[0] // 4
    lane = lax.broadcasted_iota(jnp.int32, (rows, LANES), 1)
    out = []
    for part in range(2):
        even = total[part * rows : (part + 1) * rows]
        odd = total[(2 + part) * rows : (3 + part) * rows]
        both = jnp.where(lane < HEAD, even, odd)
        out.append(both + pltpu.roll(both, HEAD, 1))
    return out


def store_half(ref, value, half):
    lane = lax.broadcasted_iota(jnp.int32, value.shape, 1)
    ref[0] = jnp.where(lane // HEAD == half, value, ref[0].astype(F32)).astype(ref.dtype)


def softmax_kernel(first_ref, q_ref, go_ref, key_ref, halo_ref, probs_ref, diag_ref, own_ref, back_ref):
    rows = key_ref.shape[1]
    u = lax.broadcasted_iota(jnp.int32, (rows, rows), 0)
    t = lax.broadcasted_iota(jnp.int32, (rows, rows), 1)
    later, same = u > t, u == t
    rate = HEAD ** (-0.5) * math.log2(math.e)
    shift = jnp.where(first_ref[0] == 1, -1e30, 0.0).astype(F32)
    half = pl.program_id(1)
    keys = stacked(key_ref[0], halo_ref[0], half)
    total = jnp.zeros((4 * rows, LANES), F32)
    for pair in range(q_ref.shape[1] // LANES):
        cols = slice(pair * LANES, (pair + 1) * LANES)
        scores = lax.dot_general(keys, q_ref[:, cols], NT, preferred_element_type=F32)
        weights = []
        for head in range(2):
            own = scores[2 * head * rows : (2 * head + 1) * rows]
            halo = scores[(2 * head + 1) * rows : (2 * head + 2) * rows] + shift
            mixed = jnp.where(later, halo, own)
            diag = jnp.sum(jnp.where(same, halo, 0.0), axis=0, keepdims=True)
            peak = jnp.maximum(jnp.max(mixed, axis=0, keepdims=True), diag)
            mixed = jnp.exp2((mixed - peak) * rate)
            diag = jnp.exp2((diag - peak) * rate)
            inverse = 1.0 / (jnp.sum(mixed, axis=0, keepdims=True) + diag)
            mixed = mixed * inverse
            diag = diag * inverse
            index = 2 * pair + head
            probs_ref[0, index] = mixed.astype(BF16)
            diag_ref[0, index : index + 1] = diag
            weights.append(jnp.where(later, 0.0, mixed).astype(BF16))
            weights.append(jnp.where(later, mixed, jnp.where(same, diag, 0.0)).astype(BF16))
        total += jnp.dot(
            jnp.concatenate(weights, axis=0), go_ref[:, cols], preferred_element_type=F32
        )
    own, back = folded(total)
    store_half(own_ref, own, half)
    store_half(back_ref, back, half)


def scores_kernel(
    q_ref, go_ref, key_ref, key_halo_ref, value_ref, value_halo_ref, probs_ref, diag_ref,
    gq_ref, own_ref, back_ref,
):
    rows = key_ref.shape[1]
    u = lax.broadcasted_iota(jnp.int32, (rows, rows), 0)
    t = lax.broadcasted_iota(jnp.int32, (rows, rows), 1)
    later, same = u > t, u == t
    factor = HEAD ** (-0.5)
    half = pl.program_id(1)
    keys = stacked(key_ref[0], key_halo_ref[0], half)
    keys_across = keys.astype(F32).T.astype(BF16)
    values = stacked(value_ref[0], value_halo_ref[0], half)
    total = jnp.zeros((4 * rows, LANES), F32)
    for pair in range(q_ref.shape[1] // LANES):
        cols = slice(pair * LANES, (pair + 1) * LANES)
        grads = lax.dot_general(values, go_ref[:, cols], NT, preferred_element_type=F32)
        terms = []
        for head in range(2):
            own = grads[2 * head * rows : (2 * head + 1) * rows]
            halo = grads[(2 * head + 1) * rows : (2 * head + 2) * rows]
            index = 2 * pair + head
            probs = probs_ref[0, index].astype(F32)
            diag = diag_ref[0, index : index + 1]
            mixed = jnp.where(later, halo, own)
            edge = jnp.sum(jnp.where(same, halo, 0.0), axis=0, keepdims=True)
            delta = jnp.sum(probs * mixed, axis=0, keepdims=True) + diag * edge
            mixed = probs * (mixed - delta)
            edge = diag * (edge - delta)
            terms.append(jnp.where(later, 0.0, mixed).astype(BF16))
            terms.append(jnp.where(later, mixed, jnp.where(same, edge, 0.0)).astype(BF16))
        stack = jnp.concatenate(terms, axis=0)
        total += jnp.dot(stack, q_ref[:, cols], preferred_element_type=F32)
        across = jnp.dot(keys_across, stack, preferred_element_type=F32)
        gq_ref[:, cols] = (across.T * factor).astype(BF16)
    own, back = folded(total)
    store_half(own_ref, own * factor, half)
    store_half(back_ref, back * factor, half)


def by_head(array):
    rows, width = array.shape
    return pl.BlockSpec((rows, width // KV_HEADS), lambda q, h: (0, h * QUARTERS + q))


def by_step(array):
    block = (1,) + array.shape[1:]
    return pl.BlockSpec(block, lambda q, h: (2 * q + h,) + (0,) * (len(block) - 1))


def by_quarter(array):
    block = (1,) + array.shape[1:]
    return pl.BlockSpec(block, lambda q, h: (q,) + (0,) * (len(block) - 1))


def softmax_part(first, queries, grad_out, keys, halo):
    rows, width = queries.shape
    group = width // (KV_HEADS * HEAD)
    probs = struct((KV_HEADS, group, rows, rows), BF16)
    diag = struct((KV_HEADS, group, rows), F32)
    sums = struct(keys.shape, F32)
    back = struct(keys.shape, BF16)
    return pl.pallas_call(
        softmax_kernel,
        grid=(QUARTERS, 2),
        in_specs=[SMEM] + [by_head(queries)] * 2 + [by_quarter(keys)] * 2,
        out_specs=[by_step(probs), by_step(diag), by_quarter(sums), by_quarter(back)],
        out_shape=[probs, diag, sums, back],
        compiler_params=params(),
        cost_estimate=cost(8 * rows * rows * width, queries, grad_out, probs),
        name="softmax_part",
    )(first, queries, grad_out, keys, halo)


def scores_part(queries, grad_out, keys, halo, values, value_halo, probs, diag):
    rows, width = queries.shape
    sums = struct(keys.shape, F32)
    back = struct(keys.shape, BF16)
    return pl.pallas_call(
        scores_kernel,
        grid=(QUARTERS, 2),
        in_specs=[by_head(queries)] * 2
        + [by_quarter(keys)] * 4
        + [by_step(probs), by_step(diag)],
        out_specs=[by_head(queries), by_quarter(sums), by_quarter(back)],
        out_shape=[struct(queries.shape, BF16), sums, back],
        compiler_params=params(),
        cost_estimate=cost(12 * rows * rows * width, queries, grad_out, queries, probs),
        name="scores_part",
    )(queries, grad_out, keys, halo, values, value_halo, probs, diag)


def ring_source(z, steps, size):
    at = (z ^ (z >> 1)) + size - steps
    at = jnp.where(at >= size, at - size, at)
    return at ^ (at >> 1)


def project_kernel(place_ref, *refs):
    pieces, hidden = refs[:8], refs[8:12]
    weight_ref, outs = refs[12], refs[13:]
    hi, z = place_ref[0], place_ref[1]
    depth = len(pieces) // 2
    step = pieces[0].shape[0] // 2
    size = pieces[0].shape[1]
    half = weight_ref.shape[0] // 2
    for r in range(2):
        for k in range(depth):
            row = ((hi ^ r) * depth + ring_source(z, k, depth)) * step
            for kind in range(2):
                weight_ref[pl.ds(pl.multiple_of(kind * half + row, step), step), :size] = pieces[
                    r * depth + k
                ][kind * step : (kind + 1) * step, :]
    weight = weight_ref[:, :size]
    for h_ref, out_ref in zip(hidden, outs):
        across = jnp.dot(weight, h_ref[...], preferred_element_type=F32)
        out_ref[...] = across.T.astype(BF16)


def project(place, pieces, hidden):
    depth, tokens = hidden[0].shape
    cols = sum(p.shape[0] for p in pieces)
    weight = struct((cols, -(-depth // LANES) * LANES), BF16)
    out = struct((tokens, cols), BF16)
    return pl.pallas_call(
        project_kernel,
        in_specs=[SMEM] + [VMEM] * (len(pieces) + len(hidden)),
        out_specs=[VMEM] * (1 + len(hidden)),
        out_shape=[weight] + [out] * len(hidden),
        compiler_params=params(),
        cost_estimate=cost(2 * 4 * tokens * cols * depth, *hidden, weight, weight),
        name="project",
    )(place, *pieces, *hidden)


def arrange_kernel(place_ref, *refs):
    key_ref, value_ref = refs[-2:]
    for r, ref in enumerate(refs[:-2]):
        key_ref[place_ref[2] ^ r] = ref[:, :LANES]
        value_ref[place_ref[2] ^ r] = ref[:, LANES:]


def arrange(place, parts):
    out = struct((len(parts), parts[0].shape[0], LANES), BF16)
    return pl.pallas_call(
        arrange_kernel,
        in_specs=[SMEM] + [VMEM] * len(parts),
        out_specs=[VMEM] * 2,
        out_shape=[out] * 2,
        compiler_params=params(),
        cost_estimate=cost(0, out, out),
        name="arrange",
    )(place, *parts)


def natural(quarters):
    lane = lax.broadcasted_iota(jnp.int32, quarters[0].shape, 1)
    blocks = []
    for half in range(2):
        for first in range(0, QUARTERS, 2):
            left, right = quarters[first], quarters[first + 1]
            if half == 0:
                right = pltpu.roll(right, HEAD, 1)
            else:
                left = pltpu.roll(left, HEAD, 1)
            blocks.append(jnp.where(lane < HEAD, left, right))
    return blocks


def finish_kernel(place_ref, *refs):
    sums, naturals, alls, outs = refs[:4], refs[4:6], refs[6:8], refs[8:]
    for kind in range(2):
        own_ref, back_ref = sums[2 * kind : 2 * kind + 2]
        quarters = []
        for q in range(QUARTERS):
            total = (own_ref[q] + back_ref[q].astype(F32)).astype(BF16)
            alls[kind][q] = total
            quarters.append(total.astype(F32))
        for m, block in enumerate(natural(quarters)):
            naturals[kind][:, m * LANES : (m + 1) * LANES] = block.astype(BF16)
        for r, ref in enumerate(outs):
            ref[:, kind * LANES : (kind + 1) * LANES] = alls[kind][place_ref[2] ^ r]


def finish(place, key_own, key_back, value_own, value_back):
    rows = key_own.shape[1]
    wide = struct((rows, QUARTERS * LANES), BF16)
    every = struct(key_own.shape, BF16)
    part = struct((rows, 2 * LANES), BF16)
    return pl.pallas_call(
        finish_kernel,
        in_specs=[SMEM] + [VMEM] * 4,
        out_specs=[VMEM] * (4 + QUARTERS),
        out_shape=[wide, wide, every, every] + [part] * QUARTERS,
        compiler_params=params(),
        cost_estimate=cost(0, key_own, key_own),
        name="finish",
    )(place, key_own, key_back, value_own, value_back)


def spans(size, step):
    return [(at, min(step, size - at)) for at in range(0, size, step)]


def weight_grad_kernel(place_ref, *refs):
    grads, hidden = refs[:4], refs[4:8]
    outs, wide_ref = refs[8:-1], refs[-1]
    hi, z = place_ref[0], place_ref[1]
    for at, size in spans(hidden[0].shape[0], 256):
        total = jnp.zeros((size, grads[0].shape[1]), F32)
        for g_ref, h_ref in zip(grads, hidden):
            total += jnp.dot(h_ref[at : at + size, :], g_ref[...], preferred_element_type=F32)
        wide_ref[:, at : at + size] = total.T
    depth = len(outs) // 2
    step = outs[0].shape[0] // 2
    half = wide_ref.shape[0] // 2
    for r in range(2):
        for k in range(depth):
            row = ((hi ^ r) * depth + (z ^ k)) * step
            for kind in range(2):
                at = pl.multiple_of(kind * half + row, step)
                outs[r * depth + k][kind * step : (kind + 1) * step, :] = wide_ref[
                    pl.ds(at, step), :
                ].astype(BF16)


def weight_grad(place, grads, hidden, depth):
    size, tokens = hidden[0].shape
    cols = grads[0].shape[1]
    part = struct((cols // (2 * depth), size), BF16)
    return pl.pallas_call(
        weight_grad_kernel,
        in_specs=[SMEM] + [VMEM] * 8,
        out_specs=[VMEM] * (2 * depth),
        out_shape=[part] * (2 * depth),
        scratch_shapes=[pltpu.VMEM((cols, size), F32)],
        compiler_params=params(),
        cost_estimate=cost(2 * 4 * tokens * cols * size, *hidden, *hidden),
        name="weight_grad",
    )(place, *grads, *hidden)


def input_grad_kernel(place_ref, key_ref, value_ref, *refs):
    out_ref = refs[-1]
    total = jnp.zeros((key_ref.shape[1], out_ref.shape[0]), F32)
    for r, w_ref in enumerate(refs[:-1]):
        half = w_ref.shape[0] // 2
        for kind, grad_ref in enumerate((key_ref, value_ref)):
            total += jnp.dot(
                grad_ref[place_ref[2] ^ r],
                w_ref[kind * half : (kind + 1) * half, :],
                preferred_element_type=F32,
            )
    out_ref[...] = total.T.astype(BF16)


def input_grad(place, key_all, value_all, weights, size):
    cols, wide = weights[0].shape
    rows = key_all.shape[1]
    step = 512
    out = struct((size, rows), BF16)
    whole = pl.BlockSpec(key_all.shape, lambda i: (0, 0, 0))
    return pl.pallas_call(
        input_grad_kernel,
        grid=(-(-size // step),),
        in_specs=[SMEM, whole, whole]
        + [pl.BlockSpec((cols, step), lambda i: (0, i))] * len(weights),
        out_specs=pl.BlockSpec((step, rows), lambda i: (i, 0)),
        out_shape=out,
        compiler_params=params(),
        cost_estimate=cost(8 * rows * cols * size, *weights, out),
        name="input_grad",
    )(place, key_all, value_all, *weights)


def after(array, *others):
    return lax.optimization_barrier((array, *others))[0]


def flip(array, axis, by):
    return lax.ppermute(array, axis, [(i, i ^ by) for i in range(lax.axis_size(axis))])


def flip_group(array, by):
    return lax.ppermute(array, ("x", "c"), [(i, i ^ by) for i in range(QUARTERS)])


def round_ring(array):
    size = lax.axis_size("z")
    order = [i ^ (i >> 1) for i in range(size)]
    return lax.ppermute(array, "z", [(order[i], order[(i + 1) % size]) for i in range(size)])


def shifted(array, by):
    size = lax.axis_size(AXES)
    pairs = [(i, i + by) for i in range(size) if 0 <= i + by < size]
    return lax.ppermute(array, AXES, pairs)


def exchanged(parts):
    return [parts[0]] + [flip_group(parts[r], r) for r in range(1, QUARTERS)]


def fast_shards(hidden_in, queries, grad_out, key_weight, value_weight):
    size = hidden_in.shape[1]
    depth = lax.axis_size("z")
    group = lax.axis_index(("x", "c"))
    place = jnp.stack([lax.axis_index("hi"), lax.axis_index("z"), group]).astype(jnp.int32)
    first = (lax.axis_index(AXES) == 0).astype(jnp.int32).reshape(1)
    own = hidden_in.T
    x_side = flip(own, "x", 1)
    pieces = [jnp.concatenate([key_weight.T, value_weight.T], axis=0)]
    across = [flip(pieces[0], "hi", 1)]
    for k in range(1, depth):
        held = pieces[-1] if k < 3 else after(pieces[-1], across[k - 3])
        pieces.append(round_ring(held))
        across.append(flip(pieces[-1], "hi", 1))
    x_side = after(x_side, pieces[-1], across[depth - 2])
    hidden = [own, flip(own, "c", 1), x_side, flip(x_side, "c", 1)]
    mine, *parts = project(place, pieces + across, hidden)
    parts = exchanged(parts)
    keys, values = arrange(place, parts)
    key_halo, value_halo = shifted(keys, 1), shifted(values, 1)

    filled = after(mine, keys)
    x_filled = flip(filled, "x", 1)
    c_filled = flip(filled, "c", 1)
    probs, diag, value_own, value_back = softmax_part(first, queries, grad_out, keys, key_halo)
    value_back = shifted(value_back, -1)
    grad_queries, key_own, key_back = scores_part(
        queries, grad_out, keys, key_halo, values, value_halo, probs, diag
    )
    grad_keys, grad_values, key_every, value_every, *parts = finish(
        place, key_own, shifted(key_back, -1), value_own, value_back
    )
    parts = [after(part, x_filled, c_filled) for part in parts]
    weights = [mine, c_filled, x_filled, flip(x_filled, "c", 1)]
    grads = weight_grad(place, exchanged(parts), hidden, depth)
    keep, send = grads[:depth], grads[depth:]
    came = [None] * depth
    total = None
    for k in reversed(range(depth)):
        came[k] = flip(send[k], "hi", 1)
        sum_k = keep[k].astype(F32) + came[k].astype(F32)
        if k:
            sum_k = flip(sum_k.astype(BF16), "z", k).astype(F32)
        total = sum_k if total is None else total + sum_k
    key_every = after(key_every, came[depth - 2])
    grad_inputs = input_grad(place, key_every, value_every, weights, size).T
    scale = (hidden_in.shape[0] * lax.axis_size(AXES)) ** (-0.5)
    total = total * scale
    rows = total.shape[0] // 2
    return (
        grad_queries,
        grad_keys,
        grad_values,
        grad_inputs,
        total[:rows].T,
        total[rows:].T,
    )


def to_quarters(rows):
    count = rows.shape[0]
    split = rows.reshape(count, 2, QUARTERS, HEAD)
    return jnp.transpose(split, (2, 0, 1, 3)).reshape(QUARTERS, count, 2 * HEAD)


def from_quarters(quarters):
    count = quarters.shape[1]
    split = quarters.reshape(QUARTERS, count, 2, HEAD)
    return jnp.transpose(split, (1, 2, 0, 3)).reshape(count, 2 * QUARTERS * HEAD)


def plain_shards(hidden_in, queries, grad_out, key_weight, value_weight):
    key_full = lax.all_gather(key_weight.T, AXES, axis=0, tiled=True)
    value_full = lax.all_gather(value_weight.T, AXES, axis=0, tiled=True)
    first = (lax.axis_index(AXES) == 0).astype(jnp.int32).reshape(1)

    def rows_of(weight):
        rows = lax.dot_general(hidden_in, weight, NT, preferred_element_type=F32)
        return to_quarters(rows.astype(BF16))

    keys, values = rows_of(key_full), rows_of(value_full)
    key_halo, value_halo = shifted(keys, 1), shifted(values, 1)
    probs, diag, value_own, value_back = softmax_part(first, queries, grad_out, keys, key_halo)
    grad_queries, key_own, key_back = scores_part(
        queries, grad_out, keys, key_halo, values, value_halo, probs, diag
    )
    grad_keys = from_quarters(key_own + shifted(key_back, -1)).astype(BF16)
    grad_values = from_quarters(value_own + shifted(value_back, -1)).astype(BF16)
    grad_inputs = (
        jnp.dot(grad_keys, key_full, preferred_element_type=F32)
        + jnp.dot(grad_values, value_full, preferred_element_type=F32)
    ).astype(BF16)
    scale = (hidden_in.shape[0] * lax.axis_size(AXES)) ** (-0.5)

    def summed(grad):
        rows = (((0,), (0,)), ((), ()))
        part = lax.dot_general(grad, hidden_in, rows, preferred_element_type=F32)
        return (lax.psum_scatter(part, AXES, scatter_dimension=0, tiled=True) * scale).T

    return (
        grad_queries,
        grad_keys,
        grad_values,
        grad_inputs,
        summed(grad_keys),
        summed(grad_values),
    )


def solution(mesh):
    outer, inner = mesh.shape["seqa"], mesh.shape["seqb"]
    split = Mesh(mesh.devices.reshape(outer // QUARTERS, 2, 2, inner), AXES)
    cols = KV_HEADS * HEAD // (outer * inner)
    fast = outer == 2 * QUARTERS and inner == 4 and cols % SUBLANES == 0
    rows, columns = P(AXES, None), P(None, AXES)
    return jax.shard_map(
        fast_shards if fast else plain_shards,
        mesh=split,
        in_specs=(rows, rows, rows, columns, columns),
        out_specs=(rows, rows, rows, rows, columns, columns),
        check_vma=False,
    )
```

```python
import functools
import math

import jax
import jax.numpy as jnp
from jax import lax
from jax.experimental import pallas as pl
from jax.experimental.pallas import tpu as pltpu
from jax.sharding import Mesh, PartitionSpec as P

KV_HEADS = 8
HEAD = 64
WIN = 128
LANES = 128
QUARTERS = 4
SUBLANES = 16

F32 = jnp.float32
BF16 = jnp.bfloat16
NT = (((1,), (1,)), ((), ()))
AXES = ("hi", "x", "c", "z")


def params(megabytes=20):
    return pltpu.CompilerParams(vmem_limit_bytes=megabytes * 1024 * 1024)


def cost(flops, *arrays):
    size = sum(math.prod(a.shape) * a.dtype.itemsize for a in arrays)
    return pl.CostEstimate(flops=int(flops), bytes_accessed=int(size), transcendentals=0)


def struct(shape, dtype):
    return jax.ShapeDtypeStruct(shape, dtype)


VMEM = pl.BlockSpec(memory_space=pltpu.VMEM)


def entire(array):
    return pl.BlockSpec(array.shape, lambda *step: (0,) * len(array.shape))


SMEM = pl.BlockSpec(memory_space=pltpu.SMEM)


def padded_pair(block, half):
    lane = lax.broadcasted_iota(jnp.int32, block.shape, 1)
    here = jnp.where(lane // HEAD == half, block.astype(F32), 0.0)
    there = pltpu.roll(here, HEAD, 1)
    even, odd = jnp.where(half == 0, here, there), jnp.where(half == 0, there, here)
    return even.astype(BF16), odd.astype(BF16)


def stacked(own, halo, half):
    own_even, own_odd = padded_pair(own, half)
    halo_even, halo_odd = padded_pair(halo, half)
    return jnp.concatenate([own_even, halo_even, own_odd, halo_odd], axis=0)


def folded(total):
    rows = total.shape[0] // 4
    lane = lax.broadcasted_iota(jnp.int32, (rows, LANES), 1)
    out = []
    for part in range(2):
        even = total[part * rows : (part + 1) * rows]
        odd = total[(2 + part) * rows : (3 + part) * rows]
        both = jnp.where(lane < HEAD, even, odd)
        out.append(both + pltpu.roll(both, HEAD, 1))
    return out


def store_half(ref, kind, value, half):
    lane = lax.broadcasted_iota(jnp.int32, value.shape, 1)
    old = ref[0, kind].astype(F32)
    ref[0, kind] = jnp.where(lane // HEAD == half, value, old).astype(ref.dtype)


def both_triangles(rows, width, dtype):
    u = lax.broadcasted_iota(jnp.int32, (rows, width), 0).astype(dtype)
    t = (lax.broadcasted_iota(jnp.int32, (rows, width), 1) % rows).astype(dtype)
    return u > t, u == t


def pair_of_blocks(ref, at):
    return jnp.concatenate(
        [ref[:, at : at + LANES], ref[:, at + LANES : at + 2 * LANES]], axis=0
    )


def attention_kernel(first_ref, q_ref, go_ref, own_ref, halo_ref, *refs):
    gq_ref, sums_ref, back_ref = refs[-3:]
    rows = own_ref.shape[2]
    later, same = both_triangles(rows, 2 * rows, jnp.int32)
    later_low, same_low = both_triangles(rows, 2 * rows, jnp.int16)
    zero = jnp.zeros((), BF16)
    factor = HEAD ** (-0.5)
    rate = factor * math.log2(math.e)
    shift = jnp.where(first_ref[0] == 1, -1e30, 0.0).astype(F32)
    half = pl.program_id(1)
    keys = stacked(own_ref[0, 0], halo_ref[0, 0], half)
    keys_across = keys.astype(F32).T.astype(BF16)
    values = stacked(own_ref[0, 1], halo_ref[0, 1], half)
    key_total = jnp.zeros((4 * rows, LANES), F32)
    value_total = jnp.zeros((4 * rows, LANES), F32)

    def split(mixed, diag):
        mixed, diag = mixed.astype(BF16), diag.astype(BF16)
        return [
            jnp.where(later_low, zero, mixed),
            jnp.where(later_low, mixed, jnp.where(same_low, diag, zero)),
        ]

    def merged(both, head):
        own = both[2 * head * rows : (2 * head + 1) * rows]
        halo = both[(2 * head + 1) * rows : (2 * head + 2) * rows]
        mixed = jnp.where(later, halo, own)
        return mixed, jnp.sum(jnp.where(same, halo, 0.0), axis=0, keepdims=True)

    hidden = jnp.where(later, shift, 0.0)
    for step in range(q_ref.shape[1] // (2 * LANES)):
        at = step * 2 * LANES
        q_pair, go_pair = pair_of_blocks(q_ref, at), pair_of_blocks(go_ref, at)
        scores = lax.dot_general(keys, q_pair, NT, preferred_element_type=F32)
        grads = lax.dot_general(values, go_pair, NT, preferred_element_type=F32)
        weights, terms = [], []
        for head in range(2):
            probs, diag = merged(scores, head)
            probs, diag = probs + hidden, diag + shift
            peak = jnp.maximum(jnp.max(probs, axis=0, keepdims=True), diag)
            probs = jnp.exp2((probs - peak) * rate)
            diag = jnp.exp2((diag - peak) * rate)
            inverse = 1.0 / (jnp.sum(probs, axis=0, keepdims=True) + diag)
            probs = probs * inverse
            diag = diag * inverse
            weights += split(probs, diag)
            mixed, edge = merged(grads, head)
            delta = jnp.sum(probs * mixed, axis=0, keepdims=True) + diag * edge
            terms += split(probs * (mixed - delta), diag * (edge - delta))
        value_total += jnp.dot(
            jnp.concatenate(weights, axis=0), go_pair, preferred_element_type=F32
        )
        stack = jnp.concatenate(terms, axis=0)
        key_total += jnp.dot(stack, q_pair, preferred_element_type=F32)
        across = jnp.dot(keys_across, stack, preferred_element_type=F32)
        for part in range(2):
            block = across[:, part * rows : (part + 1) * rows].T * factor
            gq_ref[:, at + part * LANES : at + (part + 1) * LANES] = block.astype(BF16)
    own, back = folded(key_total * factor)
    store_half(sums_ref, 0, own, half)
    store_half(back_ref, 0, back, half)
    own, back = folded(value_total)
    store_half(sums_ref, 1, own, half)
    store_half(back_ref, 1, back, half)


def attention(first, queries, grad_out, own, halo, at=0, before=None):
    rows, width = queries.shape
    sums, back = struct(own.shape, F32), struct(own.shape, BF16)
    by_head = pl.BlockSpec((rows, width // KV_HEADS), lambda q, h: (0, h * QUARTERS + at + q))
    by_quarter = pl.BlockSpec((1,) + own.shape[1:], lambda q, h: (q, 0, 0, 0))
    more = [] if before is None else [before]
    return pl.pallas_call(
        attention_kernel,
        grid=(own.shape[0], 2),
        in_specs=[SMEM] + [by_head] * 2 + [by_quarter] * 2 + [pl.BlockSpec(memory_space=pl.ANY)] * len(more),
        out_specs=[by_head, by_quarter, by_quarter],
        out_shape=[struct(queries.shape, BF16), sums, back],
        input_output_aliases={5: 0} if more else {},
        compiler_params=params(20),
        cost_estimate=cost(5 * own.shape[0] * rows * rows * width, queries, grad_out),
        name="attention",
    )(first, queries, grad_out, own, halo, *more)


def project_kernel(place_ref, *refs):
    pieces, hidden = refs[:8], refs[8:12]
    weight_ref, outs = refs[12], refs[13:]
    hi, z = place_ref[0], place_ref[1]
    depth = len(pieces) // 2
    step = pieces[0].shape[0] // 2
    size = pieces[0].shape[1]
    half = weight_ref.shape[0] // 2
    for r in range(2):
        for k in range(depth):
            row = ((hi ^ r) * depth + (z ^ k)) * step
            for kind in range(2):
                weight_ref[pl.ds(pl.multiple_of(kind * half + row, step), step), :size] = pieces[
                    r * depth + k
                ][kind * step : (kind + 1) * step, :]
    weight = weight_ref[:, :size]
    tokens = hidden[0].shape[1]
    for at in range(0, len(hidden), 2):
        pair = jnp.concatenate([hidden[at][...], hidden[at + 1][...]], axis=1)
        across = jnp.dot(weight, pair, preferred_element_type=F32)
        for k in range(2):
            outs[at + k][...] = across[:, k * tokens : (k + 1) * tokens].T.astype(BF16)


def project(place, pieces, hidden):
    depth, tokens = hidden[0].shape
    cols = sum(p.shape[0] for p in pieces)
    weight = struct((cols, -(-depth // LANES) * LANES), BF16)
    out = struct((tokens, cols), BF16)
    return pl.pallas_call(
        project_kernel,
        in_specs=[SMEM] + [entire(a) for a in pieces + hidden],
        out_specs=[VMEM] * (1 + len(hidden)),
        out_shape=[weight] + [out] * len(hidden),
        compiler_params=params(),
        cost_estimate=cost(2 * 4 * tokens * cols * depth, *hidden, weight, weight),
        name="project",
    )(place, *pieces, *hidden)


def arrange_kernel(place_ref, *refs):
    parts, outs, all_ref = refs[:QUARTERS], refs[QUARTERS:-1], refs[-1]
    for r, ref in enumerate(parts):
        for kind in range(2):
            all_ref[place_ref[2] ^ r, kind] = ref[:, kind * LANES : (kind + 1) * LANES]
    count = outs[0].shape[0]
    for k, out_ref in enumerate(outs):
        out_ref[...] = all_ref[k * count : (k + 1) * count]


def arrange(place, parts, chunks):
    shape = (2, parts[0].shape[0], LANES)
    out = struct((QUARTERS // chunks,) + shape, BF16)
    return pl.pallas_call(
        arrange_kernel,
        in_specs=[SMEM] + [entire(p) for p in parts],
        out_specs=[entire(out)] * chunks,
        out_shape=[out] * chunks,
        scratch_shapes=[pltpu.VMEM((QUARTERS,) + shape, BF16)],
        compiler_params=params(),
        cost_estimate=cost(0, out, out),
        name="arrange",
    )(place, *parts)


def natural(quarters):
    lane = lax.broadcasted_iota(jnp.int32, quarters[0].shape, 1)
    blocks = []
    for half in range(2):
        for first in range(0, QUARTERS, 2):
            left, right = quarters[first], quarters[first + 1]
            if half == 0:
                right = pltpu.roll(right, HEAD, 1)
            else:
                left = pltpu.roll(left, HEAD, 1)
            blocks.append(jnp.where(lane < HEAD, left, right))
    return blocks


def finish_kernel(chunks, place_ref, *refs):
    sums, backs = refs[:chunks], refs[chunks : 2 * chunks]
    key_ref, value_ref, all_ref = refs[2 * chunks : 2 * chunks + 3]
    outs = refs[2 * chunks + 3 :]
    count = QUARTERS // chunks
    for kind, natural_ref in enumerate((key_ref, value_ref)):
        lanes = slice(kind * LANES, (kind + 1) * LANES)
        quarters = []
        for q in range(QUARTERS):
            own = sums[q // count][q % count, kind]
            total = (own + backs[q // count][q % count, kind].astype(F32)).astype(BF16)
            all_ref[q, :, lanes] = total
            quarters.append(total.astype(F32))
        for m, block in enumerate(natural(quarters)):
            natural_ref[:, m * LANES : (m + 1) * LANES] = block.astype(BF16)
    for r, ref in enumerate(outs):
        ref[...] = all_ref[place_ref[2] ^ r]


def finish(place, sums, backs):
    rows = sums[0].shape[2]
    wide = struct((rows, QUARTERS * LANES), BF16)
    every = struct((QUARTERS, rows, 2 * LANES), BF16)
    part = struct((rows, 2 * LANES), BF16)
    shapes = [wide, wide, every] + [part] * QUARTERS
    return pl.pallas_call(
        functools.partial(finish_kernel, len(sums)),
        in_specs=[SMEM] + [entire(a) for a in sums + backs],
        out_specs=[entire(a) for a in shapes],
        out_shape=shapes,
        compiler_params=params(),
        cost_estimate=cost(0, *sums),
        name="finish",
    )(place, *sums, *backs)


def spans(size, step):
    return [(at, min(step, size - at)) for at in range(0, size, step)]


def weight_grad_kernel(place_ref, *refs):
    grads, hidden = refs[:4], refs[4:8]
    outs, wide_ref = refs[8:-1], refs[-1]
    hi, z = place_ref[0], place_ref[1]
    for at, size in spans(hidden[0].shape[0], 256):
        total = jnp.zeros((size, grads[0].shape[1]), F32)
        for k in range(0, len(grads), 2):
            rows = jnp.concatenate([h[at : at + size, :] for h in hidden[k : k + 2]], axis=1)
            cols = jnp.concatenate([g[...] for g in grads[k : k + 2]], axis=0)
            total += jnp.dot(rows, cols, preferred_element_type=F32)
        wide_ref[:, at : at + size] = total.T
    depth = len(outs) // 2
    step = outs[0].shape[0] // 2
    half = wide_ref.shape[0] // 2
    for r in range(2):
        for k in range(depth):
            row = ((hi ^ r) * depth + (z ^ k)) * step
            for kind in range(2):
                at = pl.multiple_of(kind * half + row, step)
                outs[r * depth + k][kind * step : (kind + 1) * step, :] = wide_ref[
                    pl.ds(at, step), :
                ].astype(BF16)


def weight_grad(place, grads, hidden, depth):
    size, tokens = hidden[0].shape
    cols = grads[0].shape[1]
    part = struct((cols // (2 * depth), size), BF16)
    return pl.pallas_call(
        weight_grad_kernel,
        in_specs=[SMEM] + [entire(a) for a in grads + hidden],
        out_specs=[VMEM] * (2 * depth),
        out_shape=[part] * (2 * depth),
        scratch_shapes=[pltpu.VMEM((cols, size), F32)],
        compiler_params=params(),
        cost_estimate=cost(2 * 4 * tokens * cols * size, *hidden, *hidden),
        name="weight_grad",
    )(place, *grads, *hidden)


def input_grad_kernel(place_ref, all_ref, *refs):
    out_ref = refs[-1]
    total = jnp.zeros((all_ref.shape[1], out_ref.shape[0]), F32)
    for r, w_ref in enumerate(refs[:-1]):
        total += jnp.dot(all_ref[place_ref[2] ^ r], w_ref[...], preferred_element_type=F32)
    out_ref[...] = total.T.astype(BF16)


def input_grad(place, every, weights, size):
    cols, wide = weights[0].shape
    rows = every.shape[1]
    step = 512
    out = struct((size, rows), BF16)
    return pl.pallas_call(
        input_grad_kernel,
        grid=(-(-size // step),),
        in_specs=[SMEM, entire(every)]
        + [pl.BlockSpec((cols, step), lambda i: (0, i))] * len(weights),
        out_specs=pl.BlockSpec((step, rows), lambda i: (i, 0)),
        out_shape=out,
        compiler_params=params(),
        cost_estimate=cost(8 * rows * cols * size, *weights, out),
        name="input_grad",
    )(place, every, *weights)


def after(array, *others):
    return lax.optimization_barrier((array, *others))[0]


def flip(array, axis, by):
    return lax.ppermute(array, axis, [(i, i ^ by) for i in range(lax.axis_size(axis))])


def flip_group(array, by):
    return lax.ppermute(array, ("x", "c"), [(i, i ^ by) for i in range(QUARTERS)])


def shifted(array, by):
    size = lax.axis_size(AXES)
    pairs = [(i, i + by) for i in range(size) if 0 <= i + by < size]
    return lax.ppermute(array, AXES, pairs)


def exchanged(parts):
    return [parts[0]] + [flip_group(parts[r], r) for r in range(1, QUARTERS)]


def fast_shards(hidden_in, queries, grad_out, key_weight, value_weight):
    size = hidden_in.shape[1]
    depth = lax.axis_size("z")
    group = lax.axis_index(("x", "c"))
    place = jnp.stack([lax.axis_index("hi"), lax.axis_index("z"), group]).astype(jnp.int32)
    first = (lax.axis_index(AXES) == 0).astype(jnp.int32).reshape(1)
    pieces = [jnp.concatenate([key_weight.T, value_weight.T], axis=0)]
    own = after(hidden_in.T, pieces[0])
    x_side = flip(own, "x", 1)
    pieces += [flip(pieces[0], "z", k) for k in range(1, depth)]
    across = [flip(piece, "hi", 1) for piece in pieces]
    x_side = after(x_side, pieces[-1], *across[: depth - 1])
    hidden = [own, flip(own, "c", 1), x_side, flip(x_side, "c", 1)]
    mine, *parts = project(place, pieces + across, hidden)
    chunks = 1
    rows = arrange(place, exchanged(parts), chunks)
    filled = after(mine, *rows)
    x_filled = flip(filled, "x", 1)
    c_filled = flip(filled, "c", 1)
    halos = [shifted(part, 1) for part in rows]
    grad_queries = None
    sums, backs = [], []
    for k in range(chunks):
        grad_queries, own_sums, back = attention(
            first, queries, grad_out, rows[k], halos[k], k * rows[k].shape[0], grad_queries
        )
        sums.append(own_sums)
        backs.append(shifted(after(back, *backs), -1))
    grad_keys, grad_values, every, *parts = finish(place, sums, backs)
    parts = exchanged(parts)
    parts[0] = after(parts[0], x_filled, c_filled)
    weights = [mine, c_filled, x_filled, flip(x_filled, "c", 1)]
    grads = weight_grad(place, parts, hidden, depth)
    keep, send = grads[:depth], grads[depth:]
    grad_inputs = input_grad(place, every, weights, size)
    came = []
    total = None
    for k in reversed(range(depth)):
        came.append(flip(send[k] if k else after(send[k], came[0]), "hi", 1))
        kept = keep[k] if k else after(keep[k], grad_inputs)
        sum_k = kept.astype(F32) + came[-1].astype(F32)
        if k:
            sum_k = flip(sum_k.astype(BF16), "z", k).astype(F32)
        total = sum_k if total is None else total + sum_k
    grad_inputs = grad_inputs.T
    scale = (hidden_in.shape[0] * lax.axis_size(AXES)) ** (-0.5)
    total = total * scale
    rows = total.shape[0] // 2
    return (
        grad_queries,
        grad_keys,
        grad_values,
        grad_inputs,
        total[:rows].T,
        total[rows:].T,
    )


def to_quarters(rows):
    count = rows.shape[0]
    split = rows.reshape(count, 2, QUARTERS, HEAD)
    return jnp.transpose(split, (2, 0, 1, 3)).reshape(QUARTERS, count, 2 * HEAD)


def from_quarters(quarters):
    count = quarters.shape[1]
    split = quarters.reshape(QUARTERS, count, 2, HEAD)
    return jnp.transpose(split, (1, 2, 0, 3)).reshape(count, 2 * QUARTERS * HEAD)


def plain_shards(hidden_in, queries, grad_out, key_weight, value_weight):
    key_full = lax.all_gather(key_weight.T, AXES, axis=0, tiled=True)
    value_full = lax.all_gather(value_weight.T, AXES, axis=0, tiled=True)
    first = (lax.axis_index(AXES) == 0).astype(jnp.int32).reshape(1)

    def rows_of(weight):
        rows = lax.dot_general(hidden_in, weight, NT, preferred_element_type=F32)
        return to_quarters(rows.astype(BF16))

    own = jnp.stack([rows_of(key_full), rows_of(value_full)], axis=1)
    grad_queries, sums, back = attention(first, queries, grad_out, own, shifted(own, 1))
    sums = sums + shifted(back, -1).astype(F32)
    grad_keys = from_quarters(sums[:, 0]).astype(BF16)
    grad_values = from_quarters(sums[:, 1]).astype(BF16)
    grad_inputs = (
        jnp.dot(grad_keys, key_full, preferred_element_type=F32)
        + jnp.dot(grad_values, value_full, preferred_element_type=F32)
    ).astype(BF16)
    scale = (hidden_in.shape[0] * lax.axis_size(AXES)) ** (-0.5)

    def summed(grad):
        rows = (((0,), (0,)), ((), ()))
        part = lax.dot_general(grad, hidden_in, rows, preferred_element_type=F32)
        return (lax.psum_scatter(part, AXES, scatter_dimension=0, tiled=True) * scale).T

    return (
        grad_queries,
        grad_keys,
        grad_values,
        grad_inputs,
        summed(grad_keys),
        summed(grad_values),
    )


def solution(mesh):
    outer, inner = mesh.shape["seqa"], mesh.shape["seqb"]
    split = Mesh(mesh.devices.reshape(outer // QUARTERS, 2, 2, inner), AXES)
    cols = KV_HEADS * HEAD // (outer * inner)
    fast = outer == 2 * QUARTERS and inner == 4 and cols % SUBLANES == 0
    rows, columns = P(AXES, None), P(None, AXES)
    return jax.shard_map(
        fast_shards if fast else plain_shards,
        mesh=split,
        in_specs=(rows, rows, rows, columns, columns),
        out_specs=(rows, rows, rows, rows, columns, columns),
        check_vma=False,
    )
```

```python
import functools
import math

import jax
import jax.numpy as jnp
from jax import lax
from jax.experimental import pallas as pl
from jax.experimental.pallas import tpu as pltpu
from jax.sharding import Mesh, PartitionSpec as P

KV_HEADS = 8
HEAD = 64
WIN = 128
LANES = 128
QUARTERS = 4
SUBLANES = 16

F32 = jnp.float32
BF16 = jnp.bfloat16
NT = (((1,), (1,)), ((), ()))
AXES = ("hi", "x", "c", "z")


def params(megabytes=20):
    return pltpu.CompilerParams(vmem_limit_bytes=megabytes * 1024 * 1024)


def cost(flops, *arrays):
    size = sum(math.prod(a.shape) * a.dtype.itemsize for a in arrays)
    return pl.CostEstimate(flops=int(flops), bytes_accessed=int(size), transcendentals=0)


def struct(shape, dtype):
    return jax.ShapeDtypeStruct(shape, dtype)


VMEM = pl.BlockSpec(memory_space=pltpu.VMEM)
HBM = pl.BlockSpec(memory_space=pltpu.HBM)


def entire(array):
    return pl.BlockSpec(array.shape, lambda *step: (0,) * len(array.shape))


SMEM = pl.BlockSpec(memory_space=pltpu.SMEM)


def padded_pair(block, half):
    lane = lax.broadcasted_iota(jnp.int32, block.shape, 1)
    here = jnp.where(lane // HEAD == half, block.astype(F32), 0.0)
    there = pltpu.roll(here, HEAD, 1)
    even, odd = jnp.where(half == 0, here, there), jnp.where(half == 0, there, here)
    return even.astype(BF16), odd.astype(BF16)


def stacked(own, halo, half):
    own_even, own_odd = padded_pair(own, half)
    halo_even, halo_odd = padded_pair(halo, half)
    return jnp.concatenate([own_even, halo_even, own_odd, halo_odd], axis=0)


def folded(total):
    rows = total.shape[0] // 4
    lane = lax.broadcasted_iota(jnp.int32, (rows, LANES), 1)
    out = []
    for part in range(2):
        even = total[part * rows : (part + 1) * rows]
        odd = total[(2 + part) * rows : (3 + part) * rows]
        both = jnp.where(lane < HEAD, even, odd)
        out.append(both + pltpu.roll(both, HEAD, 1))
    return out


def store_half(ref, kind, value, half):
    lane = lax.broadcasted_iota(jnp.int32, value.shape, 1)
    old = ref[0, kind].astype(F32)
    ref[0, kind] = jnp.where(lane // HEAD == half, value, old).astype(ref.dtype)


def both_triangles(rows, width, dtype):
    u = lax.broadcasted_iota(jnp.int32, (rows, width), 0).astype(dtype)
    t = (lax.broadcasted_iota(jnp.int32, (rows, width), 1) % rows).astype(dtype)
    return u > t, u == t


def pair_of_blocks(ref, at):
    return jnp.concatenate(
        [ref[:, at : at + LANES], ref[:, at + LANES : at + 2 * LANES]], axis=0
    )


def attention_kernel(at, first_ref, queries_ref, grads_ref, own_ref, halo_ref, *refs):
    gq_ref, sums_ref, back_ref, q_buffer, go_buffer, sems = refs[-6:]
    rows = own_ref.shape[2]
    width = q_buffer.shape[2]
    now = pl.program_id(0) * 2 + pl.program_id(1)

    def fetches(turn):
        slot = turn % 2
        col = ((turn % 2) * QUARTERS + at + turn // 2) * width
        cols = pl.ds(pl.multiple_of(col, width), width)
        return [
            pltpu.make_async_copy(ref.at[:, cols], buffer.at[slot], sems.at[slot, k])
            for k, (ref, buffer) in enumerate(((queries_ref, q_buffer), (grads_ref, go_buffer)))
        ]

    @pl.when(now == 0)
    def _():
        for copy in fetches(now):
            copy.start()

    @pl.when(now + 1 < pl.num_programs(0) * 2)
    def _():
        for copy in fetches(now + 1):
            copy.start()

    for copy in fetches(now):
        copy.wait()
    q_ref, go_ref = q_buffer.at[now % 2], go_buffer.at[now % 2]
    later, same = both_triangles(rows, 2 * rows, jnp.int32)
    later_low, same_low = both_triangles(rows, 2 * rows, jnp.int16)
    zero = jnp.zeros((), BF16)
    factor = HEAD ** (-0.5)
    rate = factor * math.log2(math.e)
    shift = jnp.where(first_ref[0] == 1, -1e30, 0.0).astype(F32)
    half = pl.program_id(1)
    keys = stacked(own_ref[0, 0], halo_ref[0, 0], half)
    keys_across = keys.astype(F32).T.astype(BF16)
    values = stacked(own_ref[0, 1], halo_ref[0, 1], half)
    key_total = jnp.zeros((4 * rows, LANES), F32)
    value_total = jnp.zeros((4 * rows, LANES), F32)

    def split(mixed, diag):
        mixed, diag = mixed.astype(BF16), diag.astype(BF16)
        return [
            jnp.where(later_low, zero, mixed),
            jnp.where(later_low, mixed, jnp.where(same_low, diag, zero)),
        ]

    def merged(both, head):
        own = both[2 * head * rows : (2 * head + 1) * rows]
        halo = both[(2 * head + 1) * rows : (2 * head + 2) * rows]
        mixed = jnp.where(later, halo, own)
        return mixed, jnp.sum(jnp.where(same, halo, 0.0), axis=0, keepdims=True)

    hidden = jnp.where(later, shift, 0.0)
    for step in range(width // (2 * LANES)):
        left = step * 2 * LANES
        q_pair, go_pair = pair_of_blocks(q_ref, left), pair_of_blocks(go_ref, left)
        scores = lax.dot_general(keys, q_pair, NT, preferred_element_type=F32)
        grads = lax.dot_general(values, go_pair, NT, preferred_element_type=F32)
        weights, terms = [], []
        for head in range(2):
            probs, diag = merged(scores, head)
            probs, diag = probs + hidden, diag + shift
            peak = jnp.maximum(jnp.max(probs, axis=0, keepdims=True), diag)
            probs = jnp.exp2((probs - peak) * rate)
            diag = jnp.exp2((diag - peak) * rate)
            inverse = 1.0 / (jnp.sum(probs, axis=0, keepdims=True) + diag)
            probs = probs * inverse
            diag = diag * inverse
            weights += split(probs, diag)
            mixed, edge = merged(grads, head)
            delta = jnp.sum(probs * mixed, axis=0, keepdims=True) + diag * edge
            terms += split(probs * (mixed - delta), diag * (edge - delta))
        value_total += jnp.dot(
            jnp.concatenate(weights, axis=0), go_pair, preferred_element_type=F32
        )
        stack = jnp.concatenate(terms, axis=0)
        key_total += jnp.dot(stack, q_pair, preferred_element_type=F32)
        across = jnp.dot(keys_across, stack, preferred_element_type=F32)
        for part in range(2):
            block = across[:, part * rows : (part + 1) * rows].T * factor
            gq_ref[:, left + part * LANES : left + (part + 1) * LANES] = block.astype(BF16)
    own, back = folded(key_total * factor)
    store_half(sums_ref, 0, own, half)
    store_half(back_ref, 0, back, half)
    own, back = folded(value_total)
    store_half(sums_ref, 1, own, half)
    store_half(back_ref, 1, back, half)


def attention(first, queries, grad_out, own, halo, at=0, before=None):
    rows, width = queries.shape
    sums, back = struct(own.shape, F32), struct(own.shape, BF16)
    by_head = pl.BlockSpec((rows, width // KV_HEADS), lambda q, h: (0, h * QUARTERS + at + q))
    by_quarter = pl.BlockSpec((1,) + own.shape[1:], lambda q, h: (q, 0, 0, 0))
    more = [] if before is None else [before]
    return pl.pallas_call(
        functools.partial(attention_kernel, at),
        grid=(own.shape[0], 2),
        in_specs=[SMEM, HBM, HBM, by_quarter, by_quarter] + [HBM] * len(more),
        out_specs=[by_head, by_quarter, by_quarter],
        out_shape=[struct(queries.shape, BF16), sums, back],
        scratch_shapes=[
            pltpu.VMEM((2, rows, width // KV_HEADS), BF16),
            pltpu.VMEM((2, rows, width // KV_HEADS), BF16),
            pltpu.SemaphoreType.DMA((2, 2)),
        ],
        input_output_aliases={5: 0} if more else {},
        compiler_params=params(20),
        cost_estimate=cost(5 * own.shape[0] * rows * rows * width, queries, grad_out),
        name="attention",
    )(first, queries, grad_out, own, halo, *more)


def project_kernel(place_ref, *refs):
    pieces, hidden = refs[:8], refs[8:12]
    weight_ref, outs = refs[12], refs[13:]
    hi, z = place_ref[0], place_ref[1]
    depth = len(pieces) // 2
    step = pieces[0].shape[0] // 2
    size = pieces[0].shape[1]
    half = weight_ref.shape[0] // 2
    for r in range(2):
        for k in range(depth):
            row = ((hi ^ r) * depth + (z ^ k)) * step
            for kind in range(2):
                weight_ref[pl.ds(pl.multiple_of(kind * half + row, step), step), :size] = pieces[
                    r * depth + k
                ][kind * step : (kind + 1) * step, :]
    weight = weight_ref[:, :size]
    tokens = hidden[0].shape[1]
    for at in range(0, len(hidden), 2):
        pair = jnp.concatenate([hidden[at][...], hidden[at + 1][...]], axis=1)
        across = jnp.dot(weight, pair, preferred_element_type=F32)
        for k in range(2):
            outs[at + k][...] = across[:, k * tokens : (k + 1) * tokens].T.astype(BF16)


def project(place, pieces, hidden):
    depth, tokens = hidden[0].shape
    cols = sum(p.shape[0] for p in pieces)
    weight = struct((cols, -(-depth // LANES) * LANES), BF16)
    out = struct((tokens, cols), BF16)
    return pl.pallas_call(
        project_kernel,
        in_specs=[SMEM] + [entire(a) for a in pieces + hidden],
        out_specs=[VMEM] * (1 + len(hidden)),
        out_shape=[weight] + [out] * len(hidden),
        compiler_params=params(),
        cost_estimate=cost(2 * 4 * tokens * cols * depth, *hidden, weight, weight),
        name="project",
    )(place, *pieces, *hidden)


def arrange_kernel(place_ref, *refs):
    parts, outs, all_ref = refs[:QUARTERS], refs[QUARTERS:-1], refs[-1]
    for r, ref in enumerate(parts):
        for kind in range(2):
            all_ref[place_ref[2] ^ r, kind] = ref[:, kind * LANES : (kind + 1) * LANES]
    count = outs[0].shape[0]
    for k, out_ref in enumerate(outs):
        out_ref[...] = all_ref[k * count : (k + 1) * count]


def arrange(place, parts, chunks):
    shape = (2, parts[0].shape[0], LANES)
    out = struct((QUARTERS // chunks,) + shape, BF16)
    return pl.pallas_call(
        arrange_kernel,
        in_specs=[SMEM] + [entire(p) for p in parts],
        out_specs=[entire(out)] * chunks,
        out_shape=[out] * chunks,
        scratch_shapes=[pltpu.VMEM((QUARTERS,) + shape, BF16)],
        compiler_params=params(),
        cost_estimate=cost(0, out, out),
        name="arrange",
    )(place, *parts)


def natural(quarters):
    lane = lax.broadcasted_iota(jnp.int32, quarters[0].shape, 1)
    blocks = []
    for half in range(2):
        for first in range(0, QUARTERS, 2):
            left, right = quarters[first], quarters[first + 1]
            if half == 0:
                right = pltpu.roll(right, HEAD, 1)
            else:
                left = pltpu.roll(left, HEAD, 1)
            blocks.append(jnp.where(lane < HEAD, left, right))
    return blocks


def finish_kernel(chunks, place_ref, *refs):
    sums, backs = refs[:chunks], refs[chunks : 2 * chunks]
    key_ref, value_ref, all_ref = refs[2 * chunks : 2 * chunks + 3]
    outs = refs[2 * chunks + 3 :]
    count = QUARTERS // chunks
    for kind, natural_ref in enumerate((key_ref, value_ref)):
        lanes = slice(kind * LANES, (kind + 1) * LANES)
        quarters = []
        for q in range(QUARTERS):
            own = sums[q // count][q % count, kind]
            total = (own + backs[q // count][q % count, kind].astype(F32)).astype(BF16)
            all_ref[q, :, lanes] = total
            quarters.append(total.astype(F32))
        for m, block in enumerate(natural(quarters)):
            natural_ref[:, m * LANES : (m + 1) * LANES] = block.astype(BF16)
    for r, ref in enumerate(outs):
        ref[...] = all_ref[place_ref[2] ^ r]


def finish(place, sums, backs):
    rows = sums[0].shape[2]
    wide = struct((rows, QUARTERS * LANES), BF16)
    every = struct((QUARTERS, rows, 2 * LANES), BF16)
    part = struct((rows, 2 * LANES), BF16)
    shapes = [wide, wide, every] + [part] * QUARTERS
    return pl.pallas_call(
        functools.partial(finish_kernel, len(sums)),
        in_specs=[SMEM] + [entire(a) for a in sums + backs],
        out_specs=[entire(a) for a in shapes],
        out_shape=shapes,
        compiler_params=params(),
        cost_estimate=cost(0, *sums),
        name="finish",
    )(place, *sums, *backs)


def spans(size, step):
    return [(at, min(step, size - at)) for at in range(0, size, step)]


def weight_grad_kernel(place_ref, *refs):
    grads, hidden = refs[:4], refs[4:8]
    outs, wide_ref = refs[8:-1], refs[-1]
    hi, z = place_ref[0], place_ref[1]
    for at, size in spans(hidden[0].shape[0], 256):
        total = jnp.zeros((size, grads[0].shape[1]), F32)
        for k in range(0, len(grads), 2):
            rows = jnp.concatenate([h[at : at + size, :] for h in hidden[k : k + 2]], axis=1)
            cols = jnp.concatenate([g[...] for g in grads[k : k + 2]], axis=0)
            total += jnp.dot(rows, cols, preferred_element_type=F32)
        wide_ref[:, at : at + size] = total.T
    depth = len(outs) // 2
    step = outs[0].shape[0] // 2
    half = wide_ref.shape[0] // 2
    for r in range(2):
        for k in range(depth):
            row = ((hi ^ r) * depth + (z ^ k)) * step
            for kind in range(2):
                at = pl.multiple_of(kind * half + row, step)
                outs[r * depth + k][kind * step : (kind + 1) * step, :] = wide_ref[
                    pl.ds(at, step), :
                ].astype(BF16)


def weight_grad(place, grads, hidden, depth):
    size, tokens = hidden[0].shape
    cols = grads[0].shape[1]
    part = struct((cols // (2 * depth), size), BF16)
    return pl.pallas_call(
        weight_grad_kernel,
        in_specs=[SMEM] + [entire(a) for a in grads + hidden],
        out_specs=[VMEM] * (2 * depth),
        out_shape=[part] * (2 * depth),
        scratch_shapes=[pltpu.VMEM((cols, size), F32)],
        compiler_params=params(),
        cost_estimate=cost(2 * 4 * tokens * cols * size, *hidden, *hidden),
        name="weight_grad",
    )(place, *grads, *hidden)


def input_grad_kernel(place_ref, all_ref, *refs):
    out_ref = refs[-1]
    total = jnp.zeros((all_ref.shape[1], out_ref.shape[0]), F32)
    for r, w_ref in enumerate(refs[:-1]):
        total += jnp.dot(all_ref[place_ref[2] ^ r], w_ref[...], preferred_element_type=F32)
    out_ref[...] = total.T.astype(BF16)


def input_grad(place, every, weights, size):
    cols, wide = weights[0].shape
    rows = every.shape[1]
    step = 512
    out = struct((size, rows), BF16)
    return pl.pallas_call(
        input_grad_kernel,
        grid=(-(-size // step),),
        in_specs=[SMEM, entire(every)]
        + [pl.BlockSpec((cols, step), lambda i: (0, i))] * len(weights),
        out_specs=pl.BlockSpec((step, rows), lambda i: (i, 0)),
        out_shape=out,
        compiler_params=params(),
        cost_estimate=cost(8 * rows * cols * size, *weights, out),
        name="input_grad",
    )(place, every, *weights)


def after(array, *others):
    return lax.optimization_barrier((array, *others))[0]


def flip(array, axis, by):
    return lax.ppermute(array, axis, [(i, i ^ by) for i in range(lax.axis_size(axis))])


def flip_group(array, by):
    return lax.ppermute(array, ("x", "c"), [(i, i ^ by) for i in range(QUARTERS)])


def shifted(array, by):
    size = lax.axis_size(AXES)
    pairs = [(i, i + by) for i in range(size) if 0 <= i + by < size]
    return lax.ppermute(array, AXES, pairs)


def exchanged(parts):
    return [parts[0]] + [flip_group(parts[r], r) for r in range(1, QUARTERS)]


def fast_shards(hidden_in, queries, grad_out, key_weight, value_weight):
    size = hidden_in.shape[1]
    depth = lax.axis_size("z")
    group = lax.axis_index(("x", "c"))
    place = jnp.stack([lax.axis_index("hi"), lax.axis_index("z"), group]).astype(jnp.int32)
    first = (lax.axis_index(AXES) == 0).astype(jnp.int32).reshape(1)
    pieces = [jnp.concatenate([key_weight.T, value_weight.T], axis=0)]
    own = after(hidden_in.T, pieces[0])
    x_side = flip(own, "x", 1)
    pieces += [flip(pieces[0], "z", 1), flip(pieces[0], "z", 2)]
    pieces.append(flip(pieces[2], "z", 1))
    across = [flip(piece, "hi", 1) for piece in pieces]
    x_side = after(x_side, *pieces, *across[:2])
    hidden = [own, flip(own, "c", 1), x_side, flip(x_side, "c", 1)]
    mine, *parts = project(place, pieces + across, hidden)
    chunks = 1
    rows = arrange(place, exchanged(parts), chunks)
    filled = after(mine, *rows)
    x_filled = flip(filled, "x", 1)
    c_filled = flip(filled, "c", 1)
    halos = [shifted(part, 1) for part in rows]
    grad_queries = None
    sums, backs = [], []
    for k in range(chunks):
        grad_queries, own_sums, back = attention(
            first, queries, grad_out, rows[k], halos[k], k * rows[k].shape[0], grad_queries
        )
        sums.append(own_sums)
        backs.append(shifted(after(back, *backs), -1))
    grad_keys, grad_values, every, *parts = finish(place, sums, backs)
    parts = exchanged(parts)
    parts[0] = after(parts[0], x_filled, c_filled)
    weights = [mine, c_filled, x_filled, flip(x_filled, "c", 1)]
    grads = weight_grad(place, parts, hidden, depth)
    keep, send = grads[:depth], grads[depth:]
    grad_inputs = input_grad(place, every, weights, size)
    came = []
    total = None
    for k in reversed(range(depth)):
        came.append(flip(send[k] if k else after(send[k], came[0]), "hi", 1))
        kept = keep[k] if k else after(keep[k], grad_inputs)
        sum_k = kept.astype(F32) + came[-1].astype(F32)
        if k:
            sum_k = flip(sum_k.astype(BF16), "z", k).astype(F32)
        total = sum_k if total is None else total + sum_k
    grad_inputs = grad_inputs.T
    scale = (hidden_in.shape[0] * lax.axis_size(AXES)) ** (-0.5)
    total = total * scale
    rows = total.shape[0] // 2
    return (
        grad_queries,
        grad_keys,
        grad_values,
        grad_inputs,
        total[:rows].T,
        total[rows:].T,
    )


def to_quarters(rows):
    count = rows.shape[0]
    split = rows.reshape(count, 2, QUARTERS, HEAD)
    return jnp.transpose(split, (2, 0, 1, 3)).reshape(QUARTERS, count, 2 * HEAD)


def from_quarters(quarters):
    count = quarters.shape[1]
    split = quarters.reshape(QUARTERS, count, 2, HEAD)
    return jnp.transpose(split, (1, 2, 0, 3)).reshape(count, 2 * QUARTERS * HEAD)


def plain_shards(hidden_in, queries, grad_out, key_weight, value_weight):
    key_full = lax.all_gather(key_weight.T, AXES, axis=0, tiled=True)
    value_full = lax.all_gather(value_weight.T, AXES, axis=0, tiled=True)
    first = (lax.axis_index(AXES) == 0).astype(jnp.int32).reshape(1)

    def rows_of(weight):
        rows = lax.dot_general(hidden_in, weight, NT, preferred_element_type=F32)
        return to_quarters(rows.astype(BF16))

    own = jnp.stack([rows_of(key_full), rows_of(value_full)], axis=1)
    grad_queries, sums, back = attention(first, queries, grad_out, own, shifted(own, 1))
    sums = sums + shifted(back, -1).astype(F32)
    grad_keys = from_quarters(sums[:, 0]).astype(BF16)
    grad_values = from_quarters(sums[:, 1]).astype(BF16)
    grad_inputs = (
        jnp.dot(grad_keys, key_full, preferred_element_type=F32)
        + jnp.dot(grad_values, value_full, preferred_element_type=F32)
    ).astype(BF16)
    scale = (hidden_in.shape[0] * lax.axis_size(AXES)) ** (-0.5)

    def summed(grad):
        rows = (((0,), (0,)), ((), ()))
        part = lax.dot_general(grad, hidden_in, rows, preferred_element_type=F32)
        return (lax.psum_scatter(part, AXES, scatter_dimension=0, tiled=True) * scale).T

    return (
        grad_queries,
        grad_keys,
        grad_values,
        grad_inputs,
        summed(grad_keys),
        summed(grad_values),
    )


def solution(mesh):
    outer, inner = mesh.shape["seqa"], mesh.shape["seqb"]
    split = Mesh(mesh.devices.reshape(outer // QUARTERS, 2, 2, inner), AXES)
    cols = KV_HEADS * HEAD // (outer * inner)
    fast = outer == 2 * QUARTERS and inner == 4 and cols % SUBLANES == 0
    rows, columns = P(AXES, None), P(None, AXES)
    return jax.shard_map(
        fast_shards if fast else plain_shards,
        mesh=split,
        in_specs=(rows, rows, rows, columns, columns),
        out_specs=(rows, rows, rows, rows, columns, columns),
        check_vma=False,
    )
```

```python
import functools
import math

import jax
import jax.numpy as jnp
from jax import lax
from jax.experimental import pallas as pl
from jax.experimental.pallas import tpu as pltpu
from jax.sharding import Mesh, PartitionSpec as P

KV_HEADS = 8
HEAD = 64
WIN = 128
LANES = 128
QUARTERS = 4
SUBLANES = 16

F32 = jnp.float32
BF16 = jnp.bfloat16
NT = (((1,), (1,)), ((), ()))
AXES = ("hi", "x", "c", "z")


def params(megabytes=20):
    return pltpu.CompilerParams(vmem_limit_bytes=megabytes * 1024 * 1024)


def cost(flops, *arrays):
    size = sum(math.prod(a.shape) * a.dtype.itemsize for a in arrays)
    return pl.CostEstimate(flops=int(flops), bytes_accessed=int(size), transcendentals=0)


def struct(shape, dtype):
    return jax.ShapeDtypeStruct(shape, dtype)


VMEM = pl.BlockSpec(memory_space=pltpu.VMEM)
HBM = pl.BlockSpec(memory_space=pltpu.HBM)


def entire(array):
    return pl.BlockSpec(array.shape, lambda *step: (0,) * len(array.shape))


SMEM = pl.BlockSpec(memory_space=pltpu.SMEM)


def padded_pair(block, half):
    lane = lax.broadcasted_iota(jnp.int32, block.shape, 1)
    here = jnp.where(lane // HEAD == half, block.astype(F32), 0.0)
    there = pltpu.roll(here, HEAD, 1)
    even, odd = jnp.where(half == 0, here, there), jnp.where(half == 0, there, here)
    return even.astype(BF16), odd.astype(BF16)


def stacked(own, halo, half):
    own_even, own_odd = padded_pair(own, half)
    halo_even, halo_odd = padded_pair(halo, half)
    return jnp.concatenate([own_even, halo_even, own_odd, halo_odd], axis=0)


def folded(total):
    rows = total.shape[0] // 4
    lane = lax.broadcasted_iota(jnp.int32, (rows, LANES), 1)
    out = []
    for part in range(2):
        even = total[part * rows : (part + 1) * rows]
        odd = total[(2 + part) * rows : (3 + part) * rows]
        both = jnp.where(lane < HEAD, even, odd)
        out.append(both + pltpu.roll(both, HEAD, 1))
    return out


def store_half(ref, kind, value, half):
    lane = lax.broadcasted_iota(jnp.int32, value.shape, 1)
    old = ref[0, kind].astype(F32)
    ref[0, kind] = jnp.where(lane // HEAD == half, value, old).astype(ref.dtype)


def both_triangles(rows, width, dtype):
    u = lax.broadcasted_iota(jnp.int32, (rows, width), 0).astype(dtype)
    t = (lax.broadcasted_iota(jnp.int32, (rows, width), 1) % rows).astype(dtype)
    return u > t, u == t


def pair_of_blocks(ref, at):
    return jnp.concatenate(
        [ref[:, at : at + LANES], ref[:, at + LANES : at + 2 * LANES]], axis=0
    )


def attention_kernel(at, first_ref, queries_ref, grads_ref, own_ref, halo_ref, *refs):
    gq_ref, sums_ref, back_ref, q_buffer, go_buffer, sems = refs[-6:]
    rows = own_ref.shape[2]
    width = q_buffer.shape[2]
    now = pl.program_id(0) * 2 + pl.program_id(1)

    def fetches(turn):
        slot = turn % 2
        col = ((turn % 2) * QUARTERS + at + turn // 2) * width
        cols = pl.ds(pl.multiple_of(col, width), width)
        return [
            pltpu.make_async_copy(ref.at[:, cols], buffer.at[slot], sems.at[slot, k])
            for k, (ref, buffer) in enumerate(((queries_ref, q_buffer), (grads_ref, go_buffer)))
        ]

    @pl.when(now == 0)
    def _():
        for copy in fetches(now):
            copy.start()

    @pl.when(now + 1 < pl.num_programs(0) * 2)
    def _():
        for copy in fetches(now + 1):
            copy.start()

    for copy in fetches(now):
        copy.wait()
    q_ref, go_ref = q_buffer.at[now % 2], go_buffer.at[now % 2]
    later, same = both_triangles(rows, 2 * rows, jnp.int32)
    later_low, same_low = both_triangles(rows, 2 * rows, jnp.int16)
    zero = jnp.zeros((), BF16)
    factor = HEAD ** (-0.5)
    rate = factor * math.log2(math.e)
    shift = jnp.where(first_ref[0] == 1, -1e30, 0.0).astype(F32)
    half = pl.program_id(1)
    keys = stacked(own_ref[0, 0], halo_ref[0, 0], half)
    keys_across = keys.astype(F32).T.astype(BF16)
    values = stacked(own_ref[0, 1], halo_ref[0, 1], half)
    key_total = jnp.zeros((4 * rows, LANES), F32)
    value_total = jnp.zeros((4 * rows, LANES), F32)

    def split(mixed, diag):
        mixed, diag = mixed.astype(BF16), diag.astype(BF16)
        return [
            jnp.where(later_low, zero, mixed),
            jnp.where(later_low, mixed, jnp.where(same_low, diag, zero)),
        ]

    def merged(both, head):
        own = both[2 * head * rows : (2 * head + 1) * rows]
        halo = both[(2 * head + 1) * rows : (2 * head + 2) * rows]
        mixed = jnp.where(later, halo, own)
        return mixed, jnp.sum(jnp.where(same, halo, 0.0), axis=0, keepdims=True)

    hidden = jnp.where(later, shift, 0.0)
    for step in range(width // (2 * LANES)):
        left = step * 2 * LANES
        q_pair, go_pair = pair_of_blocks(q_ref, left), pair_of_blocks(go_ref, left)
        scores = lax.dot_general(keys, q_pair, NT, preferred_element_type=F32)
        grads = lax.dot_general(values, go_pair, NT, preferred_element_type=F32)
        weights, terms = [], []
        for head in range(2):
            probs, diag = merged(scores, head)
            probs, diag = probs + hidden, diag + shift
            peak = jnp.maximum(jnp.max(probs, axis=0, keepdims=True), diag)
            probs = jnp.exp2((probs - peak) * rate)
            diag = jnp.exp2((diag - peak) * rate)
            inverse = 1.0 / (jnp.sum(probs, axis=0, keepdims=True) + diag)
            probs = probs * inverse
            diag = diag * inverse
            weights += split(probs, diag)
            mixed, edge = merged(grads, head)
            delta = jnp.sum(probs * mixed, axis=0, keepdims=True) + diag * edge
            terms += split(probs * (mixed - delta), diag * (edge - delta))
        value_total += jnp.dot(
            jnp.concatenate(weights, axis=0), go_pair, preferred_element_type=F32
        )
        stack = jnp.concatenate(terms, axis=0)
        key_total += jnp.dot(stack, q_pair, preferred_element_type=F32)
        across = jnp.dot(keys_across, stack, preferred_element_type=F32)
        for part in range(2):
            block = across[:, part * rows : (part + 1) * rows].T * factor
            gq_ref[:, left + part * LANES : left + (part + 1) * LANES] = block.astype(BF16)
    own, back = folded(key_total * factor)
    store_half(sums_ref, 0, own, half)
    store_half(back_ref, 0, back, half)
    own, back = folded(value_total)
    store_half(sums_ref, 1, own, half)
    store_half(back_ref, 1, back, half)


def attention(first, queries, grad_out, own, halo, at=0, before=None):
    rows, width = queries.shape
    sums, back = struct(own.shape, F32), struct(own.shape, BF16)
    by_head = pl.BlockSpec((rows, width // KV_HEADS), lambda q, h: (0, h * QUARTERS + at + q))
    by_quarter = pl.BlockSpec((1,) + own.shape[1:], lambda q, h: (q, 0, 0, 0))
    more = [] if before is None else [before]
    return pl.pallas_call(
        functools.partial(attention_kernel, at),
        grid=(own.shape[0], 2),
        in_specs=[SMEM, HBM, HBM, by_quarter, by_quarter] + [HBM] * len(more),
        out_specs=[by_head, by_quarter, by_quarter],
        out_shape=[struct(queries.shape, BF16), sums, back],
        scratch_shapes=[
            pltpu.VMEM((2, rows, width // KV_HEADS), BF16),
            pltpu.VMEM((2, rows, width // KV_HEADS), BF16),
            pltpu.SemaphoreType.DMA((2, 2)),
        ],
        input_output_aliases={5: 0} if more else {},
        compiler_params=params(20),
        cost_estimate=cost(5 * own.shape[0] * rows * rows * width, queries, grad_out),
        name="attention",
    )(first, queries, grad_out, own, halo, *more)


def project_kernel(place_ref, *refs):
    pieces, hidden = refs[:8], refs[8:12]
    weight_ref, outs = refs[12], refs[13:]
    hi, z = place_ref[0], place_ref[1]
    depth = len(pieces) // 2
    step = pieces[0].shape[0] // 2
    size = pieces[0].shape[1]
    half = weight_ref.shape[0] // 2
    for r in range(2):
        for k in range(depth):
            row = ((hi ^ r) * depth + (z ^ k)) * step
            for kind in range(2):
                weight_ref[pl.ds(pl.multiple_of(kind * half + row, step), step), :size] = pieces[
                    r * depth + k
                ][kind * step : (kind + 1) * step, :]
    weight = weight_ref[:, :size]
    tokens = hidden[0].shape[1]
    for at in range(0, len(hidden), 2):
        pair = jnp.concatenate([hidden[at][...], hidden[at + 1][...]], axis=1)
        across = jnp.dot(weight, pair, preferred_element_type=F32)
        for k in range(2):
            outs[at + k][...] = across[:, k * tokens : (k + 1) * tokens].T.astype(BF16)


def project(place, pieces, hidden):
    depth, tokens = hidden[0].shape
    cols = sum(p.shape[0] for p in pieces)
    weight = struct((cols, -(-depth // LANES) * LANES), BF16)
    out = struct((tokens, cols), BF16)
    return pl.pallas_call(
        project_kernel,
        in_specs=[SMEM] + [entire(a) for a in pieces + hidden],
        out_specs=[VMEM] * (1 + len(hidden)),
        out_shape=[weight] + [out] * len(hidden),
        compiler_params=params(),
        cost_estimate=cost(2 * 4 * tokens * cols * depth, *hidden, weight, weight),
        name="project",
    )(place, *pieces, *hidden)


def arrange_kernel(place_ref, *refs):
    parts, outs, all_ref = refs[:QUARTERS], refs[QUARTERS:-1], refs[-1]
    for r, ref in enumerate(parts):
        for kind in range(2):
            all_ref[place_ref[2] ^ r, kind] = ref[:, kind * LANES : (kind + 1) * LANES]
    count = outs[0].shape[0]
    for k, out_ref in enumerate(outs):
        out_ref[...] = all_ref[k * count : (k + 1) * count]


def arrange(place, parts, chunks):
    shape = (2, parts[0].shape[0], LANES)
    out = struct((QUARTERS // chunks,) + shape, BF16)
    return pl.pallas_call(
        arrange_kernel,
        in_specs=[SMEM] + [entire(p) for p in parts],
        out_specs=[entire(out)] * chunks,
        out_shape=[out] * chunks,
        scratch_shapes=[pltpu.VMEM((QUARTERS,) + shape, BF16)],
        compiler_params=params(),
        cost_estimate=cost(0, out, out),
        name="arrange",
    )(place, *parts)


def natural(quarters):
    lane = lax.broadcasted_iota(jnp.int32, quarters[0].shape, 1)
    blocks = []
    for half in range(2):
        for first in range(0, QUARTERS, 2):
            left, right = quarters[first], quarters[first + 1]
            if half == 0:
                right = pltpu.roll(right, HEAD, 1)
            else:
                left = pltpu.roll(left, HEAD, 1)
            blocks.append(jnp.where(lane < HEAD, left, right))
    return blocks


def finish_kernel(chunks, place_ref, *refs):
    sums, backs = refs[:chunks], refs[chunks : 2 * chunks]
    key_ref, value_ref, all_ref = refs[2 * chunks : 2 * chunks + 3]
    outs = refs[2 * chunks + 3 :]
    count = QUARTERS // chunks
    for kind, natural_ref in enumerate((key_ref, value_ref)):
        lanes = slice(kind * LANES, (kind + 1) * LANES)
        quarters = []
        for q in range(QUARTERS):
            own = sums[q // count][q % count, kind]
            total = (own + backs[q // count][q % count, kind].astype(F32)).astype(BF16)
            all_ref[q, :, lanes] = total
            quarters.append(total.astype(F32))
        for m, block in enumerate(natural(quarters)):
            natural_ref[:, m * LANES : (m + 1) * LANES] = block.astype(BF16)
    for r, ref in enumerate(outs):
        ref[...] = all_ref[place_ref[2] ^ r]


def finish(place, sums, backs):
    rows = sums[0].shape[2]
    wide = struct((rows, QUARTERS * LANES), BF16)
    every = struct((QUARTERS, rows, 2 * LANES), BF16)
    part = struct((rows, 2 * LANES), BF16)
    shapes = [wide, wide, every] + [part] * QUARTERS
    return pl.pallas_call(
        functools.partial(finish_kernel, len(sums)),
        in_specs=[SMEM] + [entire(a) for a in sums + backs],
        out_specs=[entire(a) for a in shapes],
        out_shape=shapes,
        compiler_params=params(),
        cost_estimate=cost(0, *sums),
        name="finish",
    )(place, *sums, *backs)


def spans(size, step):
    return [(at, min(step, size - at)) for at in range(0, size, step)]


def weight_grad_kernel(place_ref, *refs):
    grads, hidden = refs[:4], refs[4:8]
    outs, wide_ref = refs[8:-1], refs[-1]
    hi, z = place_ref[0], place_ref[1]
    for at, size in spans(hidden[0].shape[0], 256):
        total = jnp.zeros((size, grads[0].shape[1]), F32)
        for k in range(0, len(grads), 2):
            rows = jnp.concatenate([h[at : at + size, :] for h in hidden[k : k + 2]], axis=1)
            cols = jnp.concatenate([g[...] for g in grads[k : k + 2]], axis=0)
            total += jnp.dot(rows, cols, preferred_element_type=F32)
        wide_ref[:, at : at + size] = total.T
    depth = len(outs) // 2
    step = outs[0].shape[0] // 2
    half = wide_ref.shape[0] // 2
    for r in range(2):
        for k in range(depth):
            row = ((hi ^ r) * depth + (z ^ k)) * step
            for kind in range(2):
                at = pl.multiple_of(kind * half + row, step)
                outs[r * depth + k][kind * step : (kind + 1) * step, :] = wide_ref[
                    pl.ds(at, step), :
                ].astype(BF16)


def weight_grad(place, grads, hidden, depth):
    size, tokens = hidden[0].shape
    cols = grads[0].shape[1]
    part = struct((cols // (2 * depth), size), BF16)
    return pl.pallas_call(
        weight_grad_kernel,
        in_specs=[SMEM] + [entire(a) for a in grads + hidden],
        out_specs=[VMEM] * (2 * depth),
        out_shape=[part] * (2 * depth),
        scratch_shapes=[pltpu.VMEM((cols, size), F32)],
        compiler_params=params(),
        cost_estimate=cost(2 * 4 * tokens * cols * size, *hidden, *hidden),
        name="weight_grad",
    )(place, *grads, *hidden)


def input_grad_kernel(place_ref, all_ref, *refs):
    out_ref = refs[-1]
    total = jnp.zeros((all_ref.shape[1], out_ref.shape[0]), F32)
    for r, w_ref in enumerate(refs[:-1]):
        total += jnp.dot(all_ref[place_ref[2] ^ r], w_ref[...], preferred_element_type=F32)
    out_ref[...] = total.T.astype(BF16)


def input_grad(place, every, weights, size):
    cols, wide = weights[0].shape
    rows = every.shape[1]
    step = 512
    out = struct((size, rows), BF16)
    return pl.pallas_call(
        input_grad_kernel,
        grid=(-(-size // step),),
        in_specs=[SMEM, entire(every)]
        + [pl.BlockSpec((cols, step), lambda i: (0, i))] * len(weights),
        out_specs=pl.BlockSpec((step, rows), lambda i: (i, 0)),
        out_shape=out,
        compiler_params=params(),
        cost_estimate=cost(8 * rows * cols * size, *weights, out),
        name="input_grad",
    )(place, every, *weights)


def after(array, *others):
    return lax.optimization_barrier((array, *others))[0]


def flip(array, axis, by):
    return lax.ppermute(array, axis, [(i, i ^ by) for i in range(lax.axis_size(axis))])


def flip_group(array, by):
    return lax.ppermute(array, ("x", "c"), [(i, i ^ by) for i in range(QUARTERS)])


def shifted(array, by):
    size = lax.axis_size(AXES)
    pairs = [(i, i + by) for i in range(size) if 0 <= i + by < size]
    return lax.ppermute(array, AXES, pairs)


def exchanged(parts):
    return [parts[0]] + [flip_group(parts[r], r) for r in range(1, QUARTERS)]


def fast_shards(hidden_in, queries, grad_out, key_weight, value_weight):
    size = hidden_in.shape[1]
    depth = lax.axis_size("z")
    group = lax.axis_index(("x", "c"))
    place = jnp.stack([lax.axis_index("hi"), lax.axis_index("z"), group]).astype(jnp.int32)
    first = (lax.axis_index(AXES) == 0).astype(jnp.int32).reshape(1)
    pieces = [jnp.concatenate([key_weight.T, value_weight.T], axis=0)]
    own = after(hidden_in.T, pieces[0])
    x_side = flip(own, "x", 1)
    pieces += [flip(pieces[0], "z", 1), flip(pieces[0], "z", 2)]
    across = [flip(pieces[0], "hi", 1)]
    pieces.append(flip(after(pieces[2], across[0]), "z", 1))
    across += [flip(piece, "hi", 1) for piece in pieces[1:]]
    x_side = after(x_side, *pieces, across[0], across[2])
    hidden = [own, flip(own, "c", 1), x_side, flip(x_side, "c", 1)]
    mine, *parts = project(place, pieces + across, hidden)
    chunks = 1
    rows = arrange(place, exchanged(parts), chunks)
    filled = after(mine, *rows)
    x_filled = flip(filled, "x", 1)
    c_filled = flip(filled, "c", 1)
    halos = [shifted(part, 1) for part in rows]
    grad_queries = None
    sums, backs = [], []
    for k in range(chunks):
        grad_queries, own_sums, back = attention(
            first, queries, grad_out, rows[k], halos[k], k * rows[k].shape[0], grad_queries
        )
        sums.append(own_sums)
        backs.append(shifted(after(back, *backs), -1))
    grad_keys, grad_values, every, *parts = finish(place, sums, backs)
    parts = exchanged(parts)
    parts[0] = after(parts[0], x_filled, c_filled)
    weights = [mine, c_filled, x_filled, flip(x_filled, "c", 1)]
    grads = weight_grad(place, parts, hidden, depth)
    keep, send = grads[:depth], grads[depth:]
    grad_inputs = input_grad(place, every, weights, size)
    came = []
    total = None
    for k in reversed(range(depth)):
        came.append(flip(send[k] if k else after(send[k], came[0]), "hi", 1))
        kept = keep[k] if k else after(keep[k], grad_inputs)
        sum_k = kept.astype(F32) + came[-1].astype(F32)
        if k:
            sum_k = flip(sum_k.astype(BF16), "z", k).astype(F32)
        total = sum_k if total is None else total + sum_k
    grad_inputs = grad_inputs.T
    scale = (hidden_in.shape[0] * lax.axis_size(AXES)) ** (-0.5)
    total = total * scale
    rows = total.shape[0] // 2
    return (
        grad_queries,
        grad_keys,
        grad_values,
        grad_inputs,
        total[:rows].T,
        total[rows:].T,
    )


def to_quarters(rows):
    count = rows.shape[0]
    split = rows.reshape(count, 2, QUARTERS, HEAD)
    return jnp.transpose(split, (2, 0, 1, 3)).reshape(QUARTERS, count, 2 * HEAD)


def from_quarters(quarters):
    count = quarters.shape[1]
    split = quarters.reshape(QUARTERS, count, 2, HEAD)
    return jnp.transpose(split, (1, 2, 0, 3)).reshape(count, 2 * QUARTERS * HEAD)


def plain_shards(hidden_in, queries, grad_out, key_weight, value_weight):
    key_full = lax.all_gather(key_weight.T, AXES, axis=0, tiled=True)
    value_full = lax.all_gather(value_weight.T, AXES, axis=0, tiled=True)
    first = (lax.axis_index(AXES) == 0).astype(jnp.int32).reshape(1)

    def rows_of(weight):
        rows = lax.dot_general(hidden_in, weight, NT, preferred_element_type=F32)
        return to_quarters(rows.astype(BF16))

    own = jnp.stack([rows_of(key_full), rows_of(value_full)], axis=1)
    grad_queries, sums, back = attention(first, queries, grad_out, own, shifted(own, 1))
    sums = sums + shifted(back, -1).astype(F32)
    grad_keys = from_quarters(sums[:, 0]).astype(BF16)
    grad_values = from_quarters(sums[:, 1]).astype(BF16)
    grad_inputs = (
        jnp.dot(grad_keys, key_full, preferred_element_type=F32)
        + jnp.dot(grad_values, value_full, preferred_element_type=F32)
    ).astype(BF16)
    scale = (hidden_in.shape[0] * lax.axis_size(AXES)) ** (-0.5)

    def summed(grad):
        rows = (((0,), (0,)), ((), ()))
        part = lax.dot_general(grad, hidden_in, rows, preferred_element_type=F32)
        return (lax.psum_scatter(part, AXES, scatter_dimension=0, tiled=True) * scale).T

    return (
        grad_queries,
        grad_keys,
        grad_values,
        grad_inputs,
        summed(grad_keys),
        summed(grad_values),
    )


def solution(mesh):
    outer, inner = mesh.shape["seqa"], mesh.shape["seqb"]
    split = Mesh(mesh.devices.reshape(outer // QUARTERS, 2, 2, inner), AXES)
    cols = KV_HEADS * HEAD // (outer * inner)
    fast = outer == 2 * QUARTERS and inner == 4 and cols % SUBLANES == 0
    rows, columns = P(AXES, None), P(None, AXES)
    return jax.shard_map(
        fast_shards if fast else plain_shards,
        mesh=split,
        in_specs=(rows, rows, rows, columns, columns),
        out_specs=(rows, rows, rows, rows, columns, columns),
        check_vma=False,
    )
```
